128 devices in a mesh: ctx: 32 (over z, x, y_lo), kvh: 4 (over y_hi, core).
Axes of the slice: x: 4, y: 4 (y_hi: 2, y_lo: 2; y = y_hi * 2 + y_lo), z: 4, core: 2. Of those that a mesh axis runs over, the one named last changes fastest.
Arguments:
- span_queries: bfloat16 [4096, 12288], P('ctx', 'kvh'), may hold values from -8 to 8, as said below
- span_keyvals: bfloat16 [2, 4096, 1024], P(None, 'ctx', 'kvh'), may hold values from -6 to 6
- prefix_keyvals: bfloat16 [2, 2048, 1024], P(None, ('ctx', 'kvh')), may hold values from -6 to 6
- offset: int32 [1], replicated, may hold values from 1024 to 2048
- decode_queries: bfloat16 [32, 12288], replicated, may hold values from -8 to 8
- private_keyvals: bfloat16 [2, 32, 1024, 1024], P(None, None, ('ctx', 'kvh')), may hold values from -6 to 6
- suffix_lengths: int32 [32], replicated, may hold values from 1 to 1024
- out_weight: bfloat16 [12288, 12288], P('kvh', 'ctx'), may hold values from -0.0546875 to 0.0546875
Outputs:
- span_attention: float32 [4096, 12288], P('ctx', 'kvh')
- relaid_span: bfloat16 [2, 4096, 1024], P(None, ('ctx', 'kvh'))
- decode_output: float32 [32, 12288], P(None, 'ctx')
The draws below stay inside these ranges and needn't reach their ends.
Inputs may be any that keep to these rules, and one draw needn't show every extreme that they name: `span_queries`: query entries.
All inputs are finite; a program needn't handle non-finite values.
Results may differ from the reference program's by a relative error of at most 0.007.
Values may be sent and summed in bfloat16 or wider, within the bound.
A program may use at most 768 MiB of HBM per device.

```python
import math
import jax
import jax.numpy as jnp
from jax import lax

D = 12288
H = 96
KVH = 8
HD = 128
B = 32
SPAN = 4096
PREFIX = 2048
PRIV = 1024


def draw_span_queries(key, part):
    key = jax.random.fold_in(key, 3)
    base = 2.5 * jax.random.truncated_normal(key, -2.4, 2.4, (SPAN, H * HD), jnp.float32)
    return base.astype(jnp.bfloat16)


def draw_decode_queries(key, part):
    key = jax.random.fold_in(key, 7)
    base = 2.5 * jax.random.truncated_normal(key, -2.4, 2.4, (B, H * HD), jnp.float32)
    return base.astype(jnp.bfloat16)


def draw_prefix_keyvals(key, part):
    key = jax.random.fold_in(key, 5)
    base = jax.random.truncated_normal(key, -6.0, 6.0, (2, PREFIX, KVH * HD), jnp.float32)
    return base.astype(jnp.bfloat16)


def set_ends(values, key, smallest, largest):
    index_at = [jax.random.randint(jax.random.fold_in(key, axis), (), 0, length) for axis, length in enumerate(values.shape)]
    widest = values.shape.index(max(values.shape))
    neighbour = index_at[:widest] + [(index_at[widest] + 1) % values.shape[widest]] + index_at[widest + 1:]
    return values.at[tuple(index_at)].set(smallest).at[tuple(neighbour)].set(largest)


def level_of(stream_key, dims, cuts, least, top_value):
    level, own = 1.0, jax.random.fold_in(stream_key, 6)
    for axis_at, shards_of in cuts:
        heights = jnp.exp(jax.random.uniform(jax.random.fold_in(own, axis_at), (shards_of,), jnp.float32, least / len(cuts), top_value / len(cuts)))
        level = level * jnp.repeat(heights, dims[axis_at] // shards_of).reshape([-1 if axis == axis_at else 1 for axis in range(len(dims))])
    return level


def gaussian(rng, extent, width, most, pieces=(), kind=jnp.bfloat16):
    drawn = jax.random.normal(rng, extent, jnp.float32) * width
    if len(pieces) > 0:
        drawn = level_of(rng, extent, pieces, -0.22, 0.18) * drawn
    return jnp.clip(drawn, min=-most, max=most).astype(kind)


def setup_inputs(seed: int = 0) -> dict:
    arg_keys = jax.random.split(jax.random.key(seed), 9)
    return {
        "span_queries": draw_span_queries(jax.random.fold_in(arg_keys[8], 71), 0),
        "span_keyvals": gaussian(arg_keys[1], (2, SPAN, KVH * HD), 1.0, 6.0, ((1, 32), (2, 4))),
        "prefix_keyvals": draw_prefix_keyvals(jax.random.fold_in(arg_keys[8], 71), 0),
        "offset": jax.random.randint(arg_keys[3], (1,), PREFIX // 2, PREFIX + 1).astype(jnp.int32),
        "decode_queries": draw_decode_queries(jax.random.fold_in(arg_keys[8], 71), 0),
        "private_keyvals": gaussian(arg_keys[5], (2, B, PRIV, KVH * HD), 1.0, 6.0, ((2, 128),)),
        "suffix_lengths": set_ends(jax.random.randint(arg_keys[6], (B,), 1, PRIV + 1), jax.random.fold_in(arg_keys[6], 1), 1, PRIV).astype(jnp.int32),
        "out_weight": gaussian(arg_keys[7], (H * HD, D), (H * HD) ** -0.5, 0.0546875, ((0, 4), (1, 32))),
    }


masked_score = -1e30


def reference(span_queries, span_keyvals, prefix_keyvals, offset, decode_queries, private_keyvals, suffix_lengths, out_weight):
    limit = offset[0]
    per_group = H // KVH
    scale = HD ** -0.5
    keyvals = jnp.concatenate([prefix_keyvals, span_keyvals], axis=1)
    total_rows = PREFIX + SPAN
    keys = keyvals[0].reshape(total_rows, KVH, HD).astype(jnp.float32)
    values = keyvals[1].reshape(total_rows, KVH, HD).astype(jnp.float32)
    positions = jnp.arange(total_rows, dtype=jnp.int32)
    in_prefix = positions < PREFIX
    prefix_ok = positions < limit
    block = math.gcd(SPAN, 128)

    def attend(inputs):
        query_block, block_start = inputs
        rows = block_start + jnp.arange(block, dtype=jnp.int32)
        allowed = jnp.where(in_prefix[None, :], prefix_ok[None, :], (positions - PREFIX)[None, :] <= rows[:, None])
        scores = jnp.einsum('qhgd,khd->hgqk', query_block.astype(jnp.float32), keys) * scale
        scores = jnp.where(allowed[None, None], scores, masked_score)
        maxima = jnp.max(scores, axis=-1, keepdims=True)
        weights = jnp.where(allowed[None, None], jnp.exp(scores - maxima), 0.0).astype(jnp.bfloat16)
        weights = lax.optimization_barrier(weights).astype(jnp.float32)
        totals = jnp.sum(weights, axis=-1)
        summed = jnp.einsum('hgqk,khd->qhgd', weights, values)
        result = summed / jnp.transpose(totals, (2, 0, 1))[..., None]
        return result.reshape(block, H * HD)

    blocks = span_queries.reshape(SPAN // block, block, KVH, per_group, HD)
    starts = jnp.arange(SPAN // block, dtype=jnp.int32) * block
    span_attention = lax.map(attend, (blocks, starts)).reshape(SPAN, H * HD)

    sample_queries = decode_queries.reshape(B, KVH, per_group, HD).astype(jnp.float32)
    shared_ok = jnp.logical_or(prefix_ok, jnp.logical_not(in_prefix))
    shared_scores = jnp.einsum('bhgd,khd->bhgk', sample_queries, keys) * scale
    shared_scores = jnp.where(shared_ok[None, None, None, :], shared_scores, masked_score)
    private_keys = private_keyvals[0].reshape(B, PRIV, KVH, HD).astype(jnp.float32)
    private_values = private_keyvals[1].reshape(B, PRIV, KVH, HD).astype(jnp.float32)
    private_ok = jnp.arange(PRIV, dtype=jnp.int32)[None, :] < suffix_lengths[:, None]
    private_scores = jnp.einsum('bhgd,brhd->bhgr', sample_queries, private_keys) * scale
    private_scores = jnp.where(private_ok[:, None, None, :], private_scores, masked_score)
    maxima = jnp.maximum(jnp.max(shared_scores, axis=-1), jnp.max(private_scores, axis=-1))[..., None]
    shared_weights = jnp.where(shared_ok[None, None, None, :], jnp.exp(shared_scores - maxima), 0.0).astype(jnp.bfloat16)
    private_weights = jnp.where(private_ok[:, None, None, :], jnp.exp(private_scores - maxima), 0.0).astype(jnp.bfloat16)
    shared_weights = lax.optimization_barrier(shared_weights).astype(jnp.float32)
    private_weights = lax.optimization_barrier(private_weights).astype(jnp.float32)
    totals = jnp.sum(shared_weights, axis=-1) + jnp.sum(private_weights, axis=-1)
    summed = jnp.einsum('bhgk,khd->bhgd', shared_weights, values) + jnp.einsum('bhgr,brhd->bhgd', private_weights, private_values)
    mixed = (summed / totals[..., None]).reshape(B, H * HD).astype(jnp.bfloat16)
    decode_output = jnp.dot(mixed, out_weight, preferred_element_type=jnp.float32)
    return (span_attention, span_keyvals, decode_output)
```

```python
import jax
import jax.numpy as jnp
from jax import lax
from jax.experimental import pallas as pl
from jax.experimental.pallas import tpu as pltpu
from jax.sharding import PartitionSpec as P

H = 96
KVH = 8
HD = 128
CTX = 32
GROUPS = 4
SAMPLES = 32
PER = H // KVH
PAD = 16
SPAN_ROWS = 128
PRE_ROWS = 64
ROWS = SPAN_ROWS + PRE_ROWS
PREFIX = 2048
LOG2E = 1.4426950408889634
SCALE = HD ** (-0.5) * LOG2E
MASKED = -1e30

MESH = pl.DeviceIdType.MESH
F32 = jnp.float32
BF16 = jnp.bfloat16


def rem(a, n):
    return lax.rem(a, jnp.int32(n))


def dot_t(a, b):
    return lax.dot_general(a, b, (((1,), (1,)), ((), ())), preferred_element_type=F32)


def dot(a, b):
    return jnp.dot(a, b, preferred_element_type=F32)


def remote(src, dst, send, recv, device):
    return pltpu.make_async_remote_copy(
        src_ref=src, dst_ref=dst, send_sem=send, recv_sem=recv, device_id=device, device_id_type=MESH
    )


def greet(devices):
    barrier = pltpu.get_barrier_semaphore()
    for device in devices:
        pl.semaphore_signal(barrier, inc=1, device_id=device, device_id_type=MESH)
    pl.semaphore_wait(barrier, len(devices))


def decode_kernel(
    limit_ref, suffix_ref, span_ref, prefix_ref, private_ref, dq_ref, w_ref,
    prefix_out, relaid_out, decode_out,
    w_buf, q_buf, qf, priv, suf, msg, inbox, mix_own, mix_all, mix_f, part, parts,
    w_sem, dq_sem, kv_send, kv_recv, own_sem, in_send, in_recv, mix_send, mix_recv, part_send, part_recv,
):
    c = lax.axis_index("ctx")
    g = lax.axis_index("kvh")
    limit = limit_ref[0]
    width = 2 * HD

    w_copy = pltpu.make_async_copy(w_ref, w_buf, w_sem)
    w_copy.start()
    dq_copy = pltpu.make_async_copy(
        dq_ref.at[:, pl.ds(pl.multiple_of(g * 2 * PER * HD, HD), 2 * PER * HD)], q_buf, dq_sem
    )
    dq_copy.start()

    barrier = pltpu.get_barrier_semaphore()
    for k in range(1, GROUPS):
        pl.semaphore_signal(barrier, inc=1, device_id=(c, rem(g + k, GROUPS)), device_id_type=MESH)

    def greet_ctx(k, carry):
        pl.semaphore_signal(barrier, inc=1, device_id=(rem(c + k, CTX), g), device_id_type=MESH)
        return carry

    lax.fori_loop(1, CTX, greet_ctx, 0)
    pl.semaphore_wait(barrier, CTX - 1 + GROUPS - 1)

    def columns(which):
        return pl.ds(pl.multiple_of(which * width, width), width)

    def rows_of(which, count):
        return pl.ds(pl.multiple_of(which * count, count), count)

    kv_copies = []
    for k in range(1, GROUPS):
        to = rem(g + k, GROUPS)
        pairs = (
            (prefix_ref.at[:, :, columns(to)], prefix_out.at[:, rows_of(g, 16), :]),
            (private_ref.at[:, :, columns(to)], priv.at[g]),
            (span_ref.at[:, rows_of(to, 32), :], relaid_out.at[:, :, columns(g)]),
        )
        for n, (src, dst) in enumerate(pairs):
            copy = remote(src, dst, kv_send.at[n, k - 1], kv_recv.at[n, k - 1], (c, to))
            copy.start()
            kv_copies.append(copy)
    own_pairs = (
        (prefix_ref.at[:, :, columns(g)], prefix_out.at[:, rows_of(g, 16), :]),
        (private_ref.at[:, :, columns(g)], priv.at[g]),
        (span_ref.at[:, rows_of(g, 32), :], relaid_out.at[:, :, columns(g)]),
    )
    own_copies = []
    for n, (src, dst) in enumerate(own_pairs):
        copy = pltpu.make_async_copy(src, dst, own_sem.at[n])
        copy.start()
        own_copies.append(copy)

    qf[...] = jnp.zeros_like(qf)
    dq_copy.wait()
    for j in range(2 * PER):
        start = (j // PER) * SAMPLES * PAD + j % PER
        qf[pl.ds(start, SAMPLES, stride=PAD), :] = q_buf[:, j * HD : (j + 1) * HD].astype(F32)

    def set_suffix(b, carry):
        suf[pl.ds(pl.multiple_of(b * 8, 8), 8), :] = jnp.full((8, HD), suffix_ref[b], jnp.int32)
        return carry

    lax.fori_loop(0, SAMPLES, set_suffix, 0)

    for copy in own_copies:
        copy.wait()
    for copy in kv_copies:
        copy.wait_recv()

    pre_pos = c * PRE_ROWS + lax.broadcasted_iota(jnp.int32, (PRE_ROWS, HD), 0)
    pre_ok = pre_pos < limit
    row_in = lax.broadcasted_iota(jnp.int32, (8 * SAMPLES, HD), 0)
    one_pre = jnp.where(pre_ok, 1.0, 0.0).astype(BF16)
    ok_priv = [(c * GROUPS + s) * 8 + (row_in & 7) < suf[...] for s in range(GROUPS)]
    keys, values = [], []
    for h in range(2):
        cols = slice(h * HD, (h + 1) * HD)
        sub = span_ref[0, 0:1, cols].astype(F32)
        key_list = [
            span_ref[0, :, cols],
            jnp.where(pre_ok, prefix_out[0, :, cols].astype(F32), sub).astype(BF16),
        ]
        value_list = [
            jnp.concatenate([span_ref[1, :, cols], jnp.ones((SPAN_ROWS, HD), BF16)], axis=1),
            jnp.concatenate(
                [jnp.where(pre_ok, prefix_out[1, :, cols].astype(F32), 0.0).astype(BF16), one_pre], axis=1
            ),
        ]
        for s in range(GROUPS):
            key_list.append(jnp.where(ok_priv[s], priv[s, 0, :, cols].astype(F32), sub).astype(BF16))
            value_list.append(
                jnp.concatenate(
                    [
                        jnp.where(ok_priv[s], priv[s, 1, :, cols].astype(F32), 0.0).astype(BF16),
                        jnp.where(ok_priv[s], 1.0, 0.0).astype(BF16),
                    ],
                    axis=1,
                )
            )
        keys.append(jnp.concatenate(key_list, axis=0))
        values.append(jnp.concatenate(value_list, axis=0))

    tile = 128
    total = ROWS + GROUPS * 8 * SAMPLES

    def partial_tile(t, carry):
        row = t * tile + lax.broadcasted_iota(jnp.int32, (tile, total), 0)
        col = lax.broadcasted_iota(jnp.int32, (tile, total), 1) - ROWS
        match = jnp.logical_or(col < 0, (row >> 4) == ((col >> 3) & (SAMPLES - 1)))
        lane = lax.broadcasted_iota(jnp.int32, (tile, HD), 1)
        stats = jnp.zeros((tile, HD), F32)
        outs = []
        for h in range(2):
            q = qf[pl.ds(pl.multiple_of(h * SAMPLES * PAD + t * tile, tile), tile), :].astype(BF16)
            s = jnp.where(match, dot_t(q, keys[h]) * SCALE, MASKED)
            top = jnp.max(s, axis=1, keepdims=True)
            weights = jnp.exp2(s - top).astype(BF16)
            acc = dot(weights, values[h])
            total_here = acc[:, HD:]
            outs.append((acc[:, :HD] / total_here).astype(BF16))
            lse = top + jnp.log2(total_here)
            high = lse.astype(BF16).astype(F32)
            middle = (lse - high).astype(BF16).astype(F32)
            low = lse - high - middle
            stats = jnp.where(lane == 3 * h, high, stats)
            stats = jnp.where(lane == 3 * h + 1, middle, stats)
            stats = jnp.where(lane == 3 * h + 2, low, stats)
        here = pl.ds(t * (tile // PAD), tile // PAD)
        msg[here, 0, :, :] = outs[0].reshape(tile // PAD, PAD, HD)
        msg[here, 1, :, :] = outs[1].reshape(tile // PAD, PAD, HD)
        msg[here, 2, :, :] = stats.astype(BF16).reshape(tile // PAD, PAD, HD)
        return carry

    lax.fori_loop(0, SAMPLES * PAD // tile, partial_tile, 0)

    def in_copy(k):
        to = rem(c + k, CTX)
        return remote(msg.at[to], inbox.at[k], in_send.at[k], in_recv.at[k], (to, g))

    def start_in(k, carry):
        in_copy(k).start()
        return carry

    def wait_in(k, carry):
        in_copy(k).wait()
        return carry

    lax.fori_loop(1, CTX, start_in, 0)
    inbox[0] = msg[c]
    lax.fori_loop(1, CTX, wait_in, 0)

    stat = inbox[:, 2, :, :].astype(F32)
    for h in range(2):
        lse = stat[:, :, 3 * h : 3 * h + 1] + stat[:, :, 3 * h + 1 : 3 * h + 2] + stat[:, :, 3 * h + 2 : 3 * h + 3]
        weight = jnp.exp2(lse - jnp.max(lse, axis=0, keepdims=True))
        mixed = jnp.sum(weight * inbox[:, h, :, :].astype(F32), axis=0) / jnp.sum(weight, axis=0)
        mix_own[h] = mixed.astype(BF16)

    def mix_copy(k):
        to = rem(c + k, CTX)
        return remote(mix_own, mix_all.at[c], mix_send.at[k], mix_recv.at[k], (to, g))

    def start_mix(k, carry):
        mix_copy(k).start()
        return carry

    def wait_mix(k, carry):
        mix_copy(k).wait()
        return carry

    lax.fori_loop(1, CTX, start_mix, 0)
    mix_all[c] = mix_own[...]
    lax.fori_loop(1, CTX, wait_mix, 0)

    mix_f[...] = mix_all[...].astype(F32).reshape(SAMPLES * 2 * PAD, HD)
    w_copy.wait()
    columns_here = w_buf.shape[1]
    product = jnp.zeros((SAMPLES, columns_here), F32)
    for j in range(2 * PER):
        start = (j // PER) * PAD + j % PER
        a = mix_f[pl.ds(start, SAMPLES, stride=2 * PAD), :].astype(BF16)
        product = product + dot(a, w_buf[j * HD : (j + 1) * HD, :])
    part[...] = product

    part_copies = []
    for k in range(1, GROUPS):
        to = rem(g + k, GROUPS)
        copy = remote(part, parts.at[g], part_send.at[k - 1], part_recv.at[k - 1], (c, to))
        copy.start()
        part_copies.append(copy)
    parts[g] = product
    for copy in part_copies:
        copy.wait()
    for copy in kv_copies:
        copy.wait_send()
    decode_out[...] = (parts[0] + parts[1]) + (parts[2] + parts[3])


def span_kernel(
    limit_ref, q_ref, span_ref, prefix_ref,
    out_ref,
    kv, kp, vp, acc, top,
    send, recv,
):
    c = lax.axis_index("ctx")
    g = lax.axis_index("kvh")
    limit = limit_ref[0]
    z, x, y = c // 8, rem(c // 2, 4), rem(c, 2)

    def at(z_, x_, y_):
        return z_ * 8 + x_ * 2 + y_

    along_z = ((at(rem(z + 1, 4), x, y), g), (at(rem(z + 3, 4), x, y), g))
    along_x = ((at(z, rem(x + 1, 4), y), g), (at(z, rem(x + 3, 4), y), g))
    along_y = (at(z, x, 1 - y), g)
    minor = (along_x, along_z)
    major = (along_z, along_x)

    for h in range(2):
        cols = slice(h * HD, (h + 1) * HD)
        kv[h, 0, :, :SPAN_ROWS, :] = span_ref[:, :, cols]
        kv[h, 0, :, SPAN_ROWS:, :] = prefix_ref[:, :, cols]

    greet((along_z[0], along_z[1], along_x[0], along_x[1], along_y))

    sent = [0, 0]
    copies = []

    def give(h, src, dst, device):
        copy = remote(kv.at[h, src], kv.at[h, dst], send.at[h, sent[h]], recv.at[h, dst], device)
        sent[h] += 1
        copy.start()
        copies.append(copy)

    def take(h, slot):
        remote(kv.at[h, slot], kv.at[h, slot], send.at[h, 0], recv.at[h, slot], along_y).wait_recv()

    def slot(big, small, last):
        return big * 8 + small * 2 + last

    def both(h, axis, src, dst_next, dst_previous):
        give(h, src, dst_next, axis[h][0])
        give(h, src, dst_previous, axis[h][1])

    def big_step(h, small, last):
        both(h, major, slot(0, small, last), slot(3, small, last), slot(1, small, last))

    for h in range(2):
        give(h, 0, slot(0, 0, 1), along_y)
    for h in range(2):
        both(h, minor, slot(0, 0, 0), slot(0, 3, 0), slot(0, 1, 0))
    for h in range(2):
        big_step(h, 0, 0)

    row = lax.broadcasted_iota(jnp.int32, (SPAN_ROWS, SPAN_ROWS), 0)
    col = lax.broadcasted_iota(jnp.int32, (SPAN_ROWS, SPAN_ROWS), 1)
    causal = col <= row
    ones = jnp.ones((SPAN_ROWS, HD), BF16)

    def query(j):
        return q_ref[:, pl.ds(pl.multiple_of(j * HD, HD), HD)]

    for h in range(2):
        key = kv[h, 0, 0, :SPAN_ROWS, :]
        value = jnp.concatenate([kv[h, 0, 1, :SPAN_ROWS, :], ones], axis=1)

        def first(j, carry, h=h, key=key, value=value):
            s = jnp.where(causal, dot_t(query(h * PER + j), key) * SCALE, MASKED)
            highest = jnp.max(s, axis=1, keepdims=True)
            weights = jnp.exp2(s - highest).astype(BF16)
            acc[h * PER + j] = dot(weights, value)
            top[h * PER + j] = jnp.broadcast_to(highest, (SPAN_ROWS, HD))
            return carry

        lax.fori_loop(0, PER, first, 0)

    for h in range(2):
        take(h, slot(0, 0, 1))
    for h in range(2):
        both(h, minor, slot(0, 0, 1), slot(0, 3, 1), slot(0, 1, 1))
    for h in range(2):
        big_step(h, 0, 1)
    for h in range(2):
        take(h, slot(0, 3, 0))
        give(h, slot(0, 3, 0), slot(0, 2, 0), minor[h][0])
        take(h, slot(0, 1, 0))
        take(h, slot(0, 1, 1))
        give(h, slot(0, 1, 1), slot(0, 2, 1), minor[h][1])
        take(h, slot(0, 3, 1))
    for h in range(2):
        big_step(h, 3, 0)
        big_step(h, 1, 0)
    for h in range(2):
        big_step(h, 3, 1)
        big_step(h, 1, 1)
    for h in range(2):
        take(h, slot(0, 2, 0))
        take(h, slot(0, 2, 1))
    for h in range(2):
        big_step(h, 2, 0)
        big_step(h, 2, 1)

    pre_row = lax.broadcasted_iota(jnp.int32, (PRE_ROWS, HD), 0)
    one = jnp.ones((SPAN_ROWS, HD), F32)

    def chunk(h, slots):
        sub = kv[h, 0, 0, 0:1, :].astype(F32)
        for n, (big, small, last) in enumerate(slots):
            s = slot(big, small, last)
            dz, dx = (big, small) if h == 0 else (small, big)
            from_c = at(rem(z + dz, 4), rem(x + dx, 4), y if last == 0 else 1 - y)
            span_ok = jnp.full((SPAN_ROWS, HD), from_c, jnp.int32) < c
            pre_ok = from_c * PRE_ROWS + pre_row < limit
            here = n * ROWS
            kp[here : here + SPAN_ROWS, :] = jnp.where(
                span_ok, kv[h, s, 0, :SPAN_ROWS, :].astype(F32), sub
            ).astype(BF16)
            vp[here : here + SPAN_ROWS, :HD] = jnp.where(
                span_ok, kv[h, s, 1, :SPAN_ROWS, :].astype(F32), 0.0
            ).astype(BF16)
            vp[here : here + SPAN_ROWS, HD:] = jnp.where(span_ok, one, 0.0).astype(BF16)
            there = here + SPAN_ROWS
            kp[there : there + PRE_ROWS, :] = jnp.where(
                pre_ok, kv[h, s, 0, SPAN_ROWS:, :].astype(F32), sub
            ).astype(BF16)
            vp[there : there + PRE_ROWS, :HD] = jnp.where(
                pre_ok, kv[h, s, 1, SPAN_ROWS:, :].astype(F32), 0.0
            ).astype(BF16)
            vp[there : there + PRE_ROWS, HD:] = jnp.where(pre_ok, 1.0, 0.0).astype(BF16)

        def step(j, carry):
            head = h * PER + j
            s = dot_t(query(head), kp[...]) * SCALE
            before = top[head]
            highest = jnp.maximum(before, jnp.max(s, axis=1, keepdims=True))
            weights = jnp.exp2(s - highest[:, :1]).astype(BF16)
            rescale = jnp.exp2(before - highest)
            acc[head] = acc[head] * jnp.concatenate([rescale, rescale], axis=1) + dot(weights, vp[...])
            top[head] = highest
            return carry

        lax.fori_loop(0, PER, step, 0)

    halves = (
        ((0, 0), (0, 1), (3, 0), (1, 0)),
        ((3, 1), (1, 1), (2, 0), (2, 1)),
    )

    def blocks(big, half):
        return [(big, small, last) for small, last in halves[half]]

    for half in range(2):
        for h in range(2):
            chunk(h, blocks(0, half))
    for half in range(2):
        for big in (3, 1):
            for h in range(2):
                for small, last in halves[half]:
                    take(h, slot(big, small, last))
                    if last == (0 if big == 3 else 1):
                        give(h, slot(big, small, last), slot(2, small, last), major[h][0 if big == 3 else 1])
        for big in (3, 1):
            for h in range(2):
                chunk(h, blocks(big, half))
    for half in range(2):
        for h in range(2):
            for small, last in halves[half]:
                take(h, slot(2, small, last))
            chunk(h, blocks(2, half))

    def finish(j, carry):
        out_ref[:, pl.ds(pl.multiple_of(j * HD, HD), HD)] = acc[j, :, :HD] / acc[j, :, HD:]
        return carry

    lax.fori_loop(0, 2 * PER, finish, 0)
    for copy in copies:
        copy.wait_send()


def shards(
    span_queries,
    span_keyvals,
    prefix_keyvals,
    offset,
    decode_queries,
    private_keyvals,
    suffix_lengths,
    out_weight,
):
    vmem = pl.BlockSpec(memory_space=pltpu.VMEM)
    smem = pl.BlockSpec(memory_space=pltpu.SMEM)
    hbm = pl.BlockSpec(memory_space=pl.ANY)
    dma = pltpu.SemaphoreType.DMA
    group = 2 * PER * HD
    wide = out_weight.shape[1]
    private = private_keyvals.reshape(2, SAMPLES * 8, KVH * HD)
    limit_bytes = 60 * 1024 * 1024
    prefix_group, relaid_span, decode_output = pl.pallas_call(
        decode_kernel,
        out_shape=(
            jax.ShapeDtypeStruct((2, PRE_ROWS, 2 * HD), BF16),
            jax.ShapeDtypeStruct((2, SPAN_ROWS // GROUPS, KVH * HD), BF16),
            jax.ShapeDtypeStruct((SAMPLES, wide), F32),
        ),
        in_specs=[smem, smem, vmem, vmem, vmem, hbm, hbm],
        out_specs=(vmem, vmem, vmem),
        scratch_shapes=[
            pltpu.VMEM((group, wide), BF16),
            pltpu.VMEM((SAMPLES, group), BF16),
            pltpu.VMEM((2 * SAMPLES * PAD, HD), F32),
            pltpu.VMEM((GROUPS, 2, SAMPLES * 8, 2 * HD), BF16),
            pltpu.VMEM((SAMPLES * 8, HD), jnp.int32),
            pltpu.VMEM((SAMPLES, 3, PAD, HD), BF16),
            pltpu.VMEM((CTX, 3, PAD, HD), BF16),
            pltpu.VMEM((2, PAD, HD), BF16),
            pltpu.VMEM((CTX, 2, PAD, HD), BF16),
            pltpu.VMEM((SAMPLES * 2 * PAD, HD), F32),
            pltpu.VMEM((SAMPLES, wide), F32),
            pltpu.VMEM((GROUPS, SAMPLES, wide), F32),
            dma, dma, dma((3, GROUPS - 1)), dma((3, GROUPS - 1)), dma((3,)),
            dma((CTX,)), dma((CTX,)), dma((CTX,)), dma((CTX,)), dma((GROUPS - 1,)), dma((GROUPS - 1,)),
        ],
        compiler_params=pltpu.CompilerParams(
            collective_id=0, has_side_effects=True, vmem_limit_bytes=limit_bytes
        ),
        name="decode",
    )(offset, suffix_lengths, span_keyvals, prefix_keyvals, private, decode_queries, out_weight)
    span_attention = pl.pallas_call(
        span_kernel,
        out_shape=jax.ShapeDtypeStruct((SPAN_ROWS, group), F32),
        in_specs=[smem, vmem, vmem, vmem],
        out_specs=vmem,
        scratch_shapes=[
            pltpu.VMEM((2, CTX, 2, ROWS, HD), BF16),
            pltpu.VMEM((4 * ROWS, HD), BF16),
            pltpu.VMEM((4 * ROWS, 2 * HD), BF16),
            pltpu.VMEM((2 * PER, SPAN_ROWS, 2 * HD), F32),
            pltpu.VMEM((2 * PER, SPAN_ROWS, HD), F32),
            dma((2, CTX)), dma((2, CTX)),
        ],
        compiler_params=pltpu.CompilerParams(
            collective_id=1, has_side_effects=True, vmem_limit_bytes=limit_bytes
        ),
        name="span",
    )(offset, span_queries, span_keyvals, prefix_group)
    return (span_attention, relaid_span, decode_output)


def solution(mesh):
    return jax.shard_map(
        shards,
        mesh=mesh,
        in_specs=(
            P("ctx", "kvh"),
            P(None, "ctx", "kvh"),
            P(None, ("ctx", "kvh"), None),
            P(),
            P(),
            P(None, None, ("ctx", "kvh"), None),
            P(),
            P("kvh", "ctx"),
        ),
        out_specs=(P("ctx", "kvh"), P(None, ("ctx", "kvh"), None), P(None, "ctx")),
        check_vma=False,
    )
```

```python
import jax
import jax.numpy as jnp
from jax import lax
from jax.experimental import pallas as pl
from jax.experimental.pallas import tpu as pltpu
from jax.sharding import PartitionSpec as P

H = 96
KVH = 8
HD = 128
CTX = 32
GROUPS = 4
SAMPLES = 32
PER = H // KVH
PAD = 16
SPAN_ROWS = 128
PRE_ROWS = 64
ROWS = SPAN_ROWS + PRE_ROWS
PREFIX = 2048
LOG2E = 1.4426950408889634
SCALE = HD ** (-0.5) * LOG2E
MASKED = -1e30
TILE = 512
TILES = 2 * PER * SPAN_ROWS // TILE
CHUNK = 8 * ROWS

MESH = pl.DeviceIdType.MESH
F32 = jnp.float32
BF16 = jnp.bfloat16


def rem(a, n):
    return lax.rem(a, jnp.int32(n))


def dot_t(a, b):
    return lax.dot_general(a, b, (((1,), (1,)), ((), ())), preferred_element_type=F32)


def dot(a, b):
    return jnp.dot(a, b, preferred_element_type=F32)


def remote(src, dst, send, recv, device):
    return pltpu.make_async_remote_copy(
        src_ref=src, dst_ref=dst, send_sem=send, recv_sem=recv, device_id=device, device_id_type=MESH
    )


def kernel(
    limit_ref, suffix_ref, q_ref, span_ref, prefix_ref, private_ref, dq_ref, w_ref,
    out_ref, relaid_out, decode_out,
    kv, kp, vp, acc, top, scores, tops, qs, prefix_group,
    w_buf, dq_buf, qf, priv, suf, msg, inbox, mix_own, mix_all, mix_f, part, parts,
    send, recv, recv_own, local, kv_send, kv_recv, own_sem,
    in_send, in_recv, mix_send, mix_recv, part_send, part_recv,
):
    c = lax.axis_index("ctx")
    g = lax.axis_index("kvh")
    limit = limit_ref[0]
    z, x, y = c // 8, rem(c // 2, 4), rem(c, 2)
    width = 2 * HD

    w_copy = pltpu.make_async_copy(w_ref, w_buf, local.at[0])
    w_copy.start()
    dq_copy = pltpu.make_async_copy(
        dq_ref.at[:, pl.ds(pl.multiple_of(g * 2 * PER * HD, HD), 2 * PER * HD)], dq_buf, local.at[1]
    )
    dq_copy.start()
    for j in range(2 * PER):
        pltpu.make_async_copy(
            q_ref.at[:, j * HD : (j + 1) * HD], qs.at[j * SPAN_ROWS : (j + 1) * SPAN_ROWS, :], local.at[2]
        ).start()

    barrier = pltpu.get_barrier_semaphore()
    for k in range(1, GROUPS):
        pl.semaphore_signal(barrier, inc=1, device_id=(c, rem(g + k, GROUPS)), device_id_type=MESH)

    def greet_ctx(k, carry):
        pl.semaphore_signal(barrier, inc=1, device_id=(rem(c + k, CTX), g), device_id_type=MESH)
        return carry

    lax.fori_loop(1, CTX, greet_ctx, 0)
    pl.semaphore_wait(barrier, CTX - 1 + GROUPS - 1)

    def at(z_, x_, y_):
        return z_ * 8 + x_ * 2 + y_

    along_z = ((at(rem(z + 1, 4), x, y), g), (at(rem(z + 3, 4), x, y), g))
    along_x = ((at(z, rem(x + 1, 4), y), g), (at(z, rem(x + 3, 4), y), g))
    along_y = (at(z, x, 1 - y), g)
    minor = (along_x, along_z)
    major = (along_z, along_x)
    sent = [0, 0]
    copies = []

    def slot(big, small, last):
        return big * 8 + small * 2 + last

    def give(h, src, dst, device, sem):
        copy = remote(src, dst, send.at[h, sent[h]], sem, device)
        sent[h] += 1
        copy.start()
        copies.append(copy)

    def give_block(h, src, dst, device):
        give(h, kv.at[h, src], kv.at[h, dst], device, recv.at[h, dst])

    own_targets = [
        (slot(0, 0, 1), lambda h: along_y),
        (slot(0, 3, 0), lambda h: minor[h][0]),
        (slot(0, 1, 0), lambda h: minor[h][1]),
        (slot(3, 0, 0), lambda h: major[h][0]),
        (slot(1, 0, 0), lambda h: major[h][1]),
    ]
    own_slots = [dst for dst, _ in own_targets]

    def take(h, s):
        if s in own_slots:
            n = own_slots.index(s)
            first = kv.at[h, s, :, :SPAN_ROWS, :]
            second = kv.at[h, s, :, SPAN_ROWS:, :]
            remote(first, first, send.at[h, 0], recv_own.at[h, n], along_y).wait_recv()
            remote(second, second, send.at[h, 0], recv.at[h, s], along_y).wait_recv()
        else:
            remote(kv.at[h, s], kv.at[h, s], send.at[h, 0], recv.at[h, s], along_y).wait_recv()

    def both(h, axis, src, dst_next, dst_previous):
        give_block(h, src, dst_next, axis[h][0])
        give_block(h, src, dst_previous, axis[h][1])

    def big_step(h, small, last):
        both(h, major, slot(0, small, last), slot(3, small, last), slot(1, small, last))

    for n, (dst, device) in enumerate(own_targets):
        for h in range(2):
            give(
                h, span_ref.at[:, :, h * HD : (h + 1) * HD], kv.at[h, dst, :, :SPAN_ROWS, :],
                device(h), recv_own.at[h, n],
            )

    def columns(which):
        return pl.ds(pl.multiple_of(which * width, width), width)

    def rows_of(which, count):
        return pl.ds(pl.multiple_of(which * count, count), count)

    kv_copies = {}

    def exchange(n, pair):
        for k in range(1, GROUPS):
            to = rem(g + k, GROUPS)
            src, dst = pair(to)
            copy = remote(src, dst, kv_send.at[n, k - 1], kv_recv.at[n, k - 1], (c, to))
            copy.start()
            kv_copies[n, k] = copy
        src, dst = pair(g)
        copy = pltpu.make_async_copy(src, dst, own_sem.at[n])
        copy.start()
        kv_copies[n, 0] = copy

    def received(n):
        kv_copies[n, 0].wait()
        for k in range(1, GROUPS):
            kv_copies[n, k].wait_recv()

    exchange(0, lambda to: (prefix_ref.at[:, :, columns(to)], prefix_group.at[:, rows_of(g, 16), :]))
    exchange(1, lambda to: (span_ref.at[:, rows_of(to, 32), :], relaid_out.at[:, :, columns(g)]))

    pltpu.make_async_copy(qs, qs, local.at[2]).wait()
    row = lax.broadcasted_iota(jnp.int32, (SPAN_ROWS, SPAN_ROWS), 0)
    col = lax.broadcasted_iota(jnp.int32, (SPAN_ROWS, SPAN_ROWS), 1)
    allowed = jnp.concatenate([col <= row] * (TILE // SPAN_ROWS), axis=0)
    ones = jnp.ones((SPAN_ROWS, HD), BF16)
    for h in range(2):
        cols = slice(h * HD, (h + 1) * HD)
        kv[h, 0, :, :SPAN_ROWS, :] = span_ref[:, :, cols]

    def tile_rows(t):
        return pl.ds(pl.multiple_of(t * TILE, TILE), TILE)

    def first(t, carry):
        h = t // (TILES // 2)
        s = jnp.where(allowed, dot_t(qs[tile_rows(t), :], kv[h, 0, 0, :SPAN_ROWS, :]) * SCALE, MASKED)
        highest = jnp.broadcast_to(jnp.max(s, axis=1, keepdims=True), (TILE, HD))
        weights = jnp.exp2(s - highest).astype(BF16)
        acc[t] = dot(weights, jnp.concatenate([kv[h, 0, 1, :SPAN_ROWS, :], ones], axis=1))
        top[t] = highest
        return carry

    lax.fori_loop(0, TILES, first, 0)

    received(0)
    for h in range(2):
        cols = slice(h * HD, (h + 1) * HD)
        kv[h, 0, :, SPAN_ROWS:, :] = prefix_group[:, :, cols]
    for n, (dst, device) in enumerate(own_targets):
        for h in range(2):
            give(
                h, kv.at[h, 0, :, SPAN_ROWS:, :], kv.at[h, dst, :, SPAN_ROWS:, :], device(h), recv.at[h, dst]
            )
    for h in range(2):
        take(h, slot(0, 0, 1))
        both(h, minor, slot(0, 0, 1), slot(0, 3, 1), slot(0, 1, 1))
        big_step(h, 0, 1)
    exchange(2, lambda to: (private_ref.at[:, :, columns(to)], priv.at[g]))

    qf[...] = jnp.zeros_like(qf)
    dq_copy.wait()
    for j in range(2 * PER):
        start = (j // PER) * SAMPLES * PAD + j % PER
        qf[pl.ds(start, SAMPLES, stride=PAD), :] = dq_buf[:, j * HD : (j + 1) * HD].astype(F32)

    def set_suffix(b, carry):
        suf[pl.ds(pl.multiple_of(b * 8, 8), 8), :] = jnp.full((8, HD), suffix_ref[b], jnp.int32)
        return carry

    lax.fori_loop(0, SAMPLES, set_suffix, 0)

    for h in range(2):
        take(h, slot(0, 3, 0))
        give_block(h, slot(0, 3, 0), slot(0, 2, 0), minor[h][0])
        take(h, slot(0, 1, 0))
        take(h, slot(0, 1, 1))
        give_block(h, slot(0, 1, 1), slot(0, 2, 1), minor[h][1])
        take(h, slot(0, 3, 1))
    for h in range(2):
        big_step(h, 3, 0)
        big_step(h, 1, 0)
    for h in range(2):
        big_step(h, 3, 1)
        big_step(h, 1, 1)
    for h in range(2):
        take(h, slot(0, 2, 0))
        take(h, slot(0, 2, 1))
    for h in range(2):
        big_step(h, 2, 0)
        big_step(h, 2, 1)

    pre_row = lax.broadcasted_iota(jnp.int32, (PRE_ROWS, HD), 0)

    def put(h, here, count, ok, key, value, sub):
        kp[h, here : here + count, :] = jnp.where(ok, key.astype(F32), sub).astype(BF16)
        vp[h, here : here + count, :HD] = jnp.where(ok, value.astype(F32), 0.0).astype(BF16)
        vp[h, here : here + count, HD:] = jnp.where(ok, 1.0, 0.0).astype(BF16)

    def score(t, n, half):
        h = t // (TILES // 2)
        q = qs[tile_rows(t), :]
        most = None
        for a in range(0, n, 2 * HD):
            s = dot_t(q, kp[h, a : a + 2 * HD, :])
            scores[half, :, a : a + 2 * HD] = s
            here = jnp.maximum(s[:, :HD], s[:, HD:])
            most = here if most is None else jnp.maximum(most, here)
        tops[half] = most

    def weigh(t, n, half):
        h = t // (TILES // 2)
        before = top[t]
        highest = jnp.maximum(
            before, jnp.broadcast_to(jnp.max(tops[half], axis=1, keepdims=True) * SCALE, (TILE, HD))
        )
        rescale = jnp.exp2(before - highest)
        top[t] = highest
        weights = jnp.concatenate(
            [
                jnp.exp2(scores[half, :, a : a + HD] * SCALE - highest).astype(BF16)
                for a in range(0, n, HD)
            ],
            axis=1,
        )
        acc[t] = acc[t] * jnp.concatenate([rescale, rescale], axis=1) + dot(weights, vp[h, :n, :])

    def chunk(blocks):
        size = len(blocks) * ROWS
        for h in range(2):
            sub = kv[h, 0, 0, 0:1, :].astype(F32)
            for n, (big, small, last) in enumerate(blocks):
                s = slot(big, small, last)
                dz, dx = (big, small) if h == 0 else (small, big)
                from_c = at(rem(z + dz, 4), rem(x + dx, 4), y if last == 0 else 1 - y)
                span_ok = jnp.full((SPAN_ROWS, HD), from_c, jnp.int32) < c
                pre_ok = from_c * PRE_ROWS + pre_row < limit
                here = n * ROWS
                put(h, here, SPAN_ROWS, span_ok, kv[h, s, 0, :SPAN_ROWS, :], kv[h, s, 1, :SPAN_ROWS, :], sub)
                put(
                    h, here + SPAN_ROWS, PRE_ROWS, pre_ok, kv[h, s, 0, SPAN_ROWS:, :], kv[h, s, 1, SPAN_ROWS:, :], sub
                )
        score(0, size, 0)

        def two(i, carry):
            score(2 * i + 1, size, 1)
            weigh(2 * i, size, 0)
            score(2 * i + 2, size, 0)
            weigh(2 * i + 1, size, 1)
            return carry

        lax.fori_loop(0, TILES // 2 - 1, two, 0)
        score(TILES - 1, size, 1)
        weigh(TILES - 2, size, 0)
        weigh(TILES - 1, size, 1)

    halves = (
        ((0, 0), (0, 1), (3, 0), (1, 0)),
        ((3, 1), (1, 1), (2, 0), (2, 1)),
    )

    def pass_on(half):
        for small, last in halves[half]:
            for h in range(2):
                for big in (3, 1):
                    take(h, slot(big, small, last))
                    if last == (0 if big == 3 else 1):
                        give_block(
                            h, slot(big, small, last), slot(2, small, last), major[h][0 if big == 3 else 1]
                        )

    chunk([(0, small, last) for half in halves for small, last in half])
    pass_on(0)

    received(2)
    pre_pos = c * PRE_ROWS + pre_row
    row_in = lax.broadcasted_iota(jnp.int32, (8 * SAMPLES, HD), 0)
    always = jnp.full((SPAN_ROWS, HD), True)
    total = ROWS + GROUPS * 8 * SAMPLES
    rows = SAMPLES * PAD
    for h in range(2):
        cols = slice(h * HD, (h + 1) * HD)
        sub = span_ref[0, 0:1, cols].astype(F32)
        kp[h, :SPAN_ROWS, :] = span_ref[0, :, cols]
        vp[h, :SPAN_ROWS, :HD] = span_ref[1, :, cols]
        vp[h, :SPAN_ROWS, HD:] = ones
        put(h, SPAN_ROWS, PRE_ROWS, pre_pos < limit, prefix_group[0, :, cols], prefix_group[1, :, cols], sub)
        for s in range(GROUPS):
            ok = (c * GROUPS + s) * 8 + (row_in & 7) < suf[...]
            put(h, ROWS + s * 8 * SAMPLES, 8 * SAMPLES, ok, priv[s, 0, :, cols], priv[s, 1, :, cols], sub)
    lane = lax.broadcasted_iota(jnp.int32, (rows, HD), 1)
    own_sample = lax.broadcasted_iota(jnp.int32, (rows, HD), 0) >> 4
    stats = jnp.zeros((rows, HD), F32)
    for h in range(2):
        q = qf[h * rows : (h + 1) * rows, :].astype(BF16)
        most = None
        spans = [(0, ROWS, False)] + [(ROWS + s * 256, 256, True) for s in range(GROUPS)]
        for start, count, masked in spans:
            s = dot_t(q, kp[h, start : start + count, :]) * SCALE
            if masked:
                key_sample = lax.broadcasted_iota(jnp.int32, (rows, count), 1) >> 3
                query_sample = lax.broadcasted_iota(jnp.int32, (rows, count), 0) >> 4
                s = jnp.where(key_sample == query_sample, s, MASKED)
            scores[h, :, start : start + count] = s
            here = jnp.max(s, axis=1, keepdims=True)
            most = here if most is None else jnp.maximum(most, here)
        weights = jnp.exp2(scores[h, :, :total] - most).astype(BF16)
        both_sums = dot(weights, vp[h, :total, :])
        total_here = both_sums[:, HD:]
        msg[:, h, :, :] = (both_sums[:, :HD] / total_here).astype(BF16).reshape(SAMPLES, PAD, HD)
        lse = most + jnp.log2(total_here)
        high = lse.astype(BF16).astype(F32)
        middle = (lse - high).astype(BF16).astype(F32)
        low = lse - high - middle
        stats = jnp.where(lane == 3 * h, high, stats)
        stats = jnp.where(lane == 3 * h + 1, middle, stats)
        stats = jnp.where(lane == 3 * h + 2, low, stats)
    msg[:, 2, :, :] = stats.astype(BF16).reshape(SAMPLES, PAD, HD)

    def in_copy(k):
        to = rem(c + k, CTX)
        return remote(msg.at[to], inbox.at[k], in_send.at[k], in_recv.at[k], (to, g))

    def mix_copy(k):
        to = rem(c + k, CTX)
        return remote(mix_own, mix_all.at[c], mix_send.at[k], mix_recv.at[k], (to, g))

    def start_in(k, carry):
        in_copy(k).start()
        return carry

    def wait_in(k, carry):
        in_copy(k).wait()
        return carry

    def start_mix(k, carry):
        mix_copy(k).start()
        return carry

    def wait_mix(k, carry):
        mix_copy(k).wait()
        return carry

    lax.fori_loop(1, CTX, start_in, 0)
    inbox[0] = msg[c]

    chunk([(big, small, last) for big in (3, 1) for small, last in halves[0]])
    pass_on(1)

    lax.fori_loop(1, CTX, wait_in, 0)
    stat = inbox[:, 2, :, :].astype(F32)
    for h in range(2):
        lse = stat[:, :, 3 * h : 3 * h + 1] + stat[:, :, 3 * h + 1 : 3 * h + 2] + stat[:, :, 3 * h + 2 : 3 * h + 3]
        weight = jnp.exp2(lse - jnp.max(lse, axis=0, keepdims=True))
        mixed = jnp.sum(weight * inbox[:, h, :, :].astype(F32), axis=0) / jnp.sum(weight, axis=0)
        mix_own[h] = mixed.astype(BF16)
    lax.fori_loop(1, CTX, start_mix, 0)
    mix_all[c] = mix_own[...]

    chunk([(big, small, last) for big in (3, 1) for small, last in halves[1]])

    lax.fori_loop(1, CTX, wait_mix, 0)
    mix_f[...] = mix_all[...].astype(F32).reshape(SAMPLES * 2 * PAD, HD)
    w_copy.wait()
    columns_here = w_buf.shape[1]
    product = jnp.zeros((SAMPLES, columns_here), F32)
    for j in range(2 * PER):
        start = (j // PER) * PAD + j % PER
        a = mix_f[pl.ds(start, SAMPLES, stride=2 * PAD), :].astype(BF16)
        product = product + dot(a, w_buf[j * HD : (j + 1) * HD, :])
    part[...] = product
    part_copies = []
    for k in range(1, GROUPS):
        to = rem(g + k, GROUPS)
        copy = remote(part, parts.at[g], part_send.at[k - 1], part_recv.at[k - 1], (c, to))
        copy.start()
        part_copies.append(copy)
    parts[g] = product

    for half in range(2):
        for small, last in halves[half]:
            for h in range(2):
                take(h, slot(2, small, last))
        chunk([(2, small, last) for small, last in halves[half]])

    for j in range(2 * PER):
        t, r = j * SPAN_ROWS // TILE, j * SPAN_ROWS % TILE
        here = slice(r, r + SPAN_ROWS)
        out_ref[:, j * HD : (j + 1) * HD] = acc[t, here, :HD] / acc[t, here, HD:]

    for copy in part_copies:
        copy.wait()
    decode_out[...] = (parts[0] + parts[1]) + (parts[2] + parts[3])
    received(1)
    for (n, k), copy in kv_copies.items():
        if k:
            copy.wait_send()
    for copy in copies:
        copy.wait_send()


def shards(
    span_queries,
    span_keyvals,
    prefix_keyvals,
    offset,
    decode_queries,
    private_keyvals,
    suffix_lengths,
    out_weight,
):
    vmem = pl.BlockSpec(memory_space=pltpu.VMEM)
    smem = pl.BlockSpec(memory_space=pltpu.SMEM)
    hbm = pl.BlockSpec(memory_space=pl.ANY)
    dma = pltpu.SemaphoreType.DMA
    group = 2 * PER * HD
    wide = out_weight.shape[1]
    private = private_keyvals.reshape(2, SAMPLES * 8, KVH * HD)
    return pl.pallas_call(
        kernel,
        out_shape=(
            jax.ShapeDtypeStruct((SPAN_ROWS, group), F32),
            jax.ShapeDtypeStruct((2, SPAN_ROWS // GROUPS, KVH * HD), BF16),
            jax.ShapeDtypeStruct((SAMPLES, wide), F32),
        ),
        in_specs=[smem, smem, hbm, vmem, vmem, hbm, hbm, hbm],
        out_specs=(vmem, vmem, vmem),
        scratch_shapes=[
            pltpu.VMEM((2, CTX, 2, ROWS, HD), BF16),
            pltpu.VMEM((2, CHUNK, HD), BF16),
            pltpu.VMEM((2, CHUNK, 2 * HD), BF16),
            pltpu.VMEM((TILES, TILE, 2 * HD), F32),
            pltpu.VMEM((TILES, TILE, HD), F32),
            pltpu.VMEM((2, TILE, CHUNK), F32),
            pltpu.VMEM((2, TILE, HD), F32),
            pltpu.VMEM((group, HD), BF16),
            pltpu.VMEM((2, PRE_ROWS, 2 * HD), BF16),
            pltpu.VMEM((group, wide), BF16),
            pltpu.VMEM((SAMPLES, group), BF16),
            pltpu.VMEM((2 * SAMPLES * PAD, HD), F32),
            pltpu.VMEM((GROUPS, 2, SAMPLES * 8, 2 * HD), BF16),
            pltpu.VMEM((SAMPLES * 8, HD), jnp.int32),
            pltpu.VMEM((SAMPLES, 3, PAD, HD), BF16),
            pltpu.VMEM((CTX, 3, PAD, HD), BF16),
            pltpu.VMEM((2, PAD, HD), BF16),
            pltpu.VMEM((CTX, 2, PAD, HD), BF16),
            pltpu.VMEM((SAMPLES * 2 * PAD, HD), F32),
            pltpu.VMEM((SAMPLES, wide), F32),
            pltpu.VMEM((GROUPS, SAMPLES, wide), F32),
            dma((2, 40)), dma((2, CTX)), dma((2, 5)), dma((3,)),
            dma((3, GROUPS - 1)), dma((3, GROUPS - 1)), dma((3,)),
            dma((CTX,)), dma((CTX,)), dma((CTX,)), dma((CTX,)), dma((GROUPS - 1,)), dma((GROUPS - 1,)),
        ],
        compiler_params=pltpu.CompilerParams(
            collective_id=0, has_side_effects=True, vmem_limit_bytes=60 * 1024 * 1024
        ),
        name="attention",
    )(offset, suffix_lengths, span_queries, span_keyvals, prefix_keyvals, private, decode_queries, out_weight)


def solution(mesh):
    return jax.shard_map(
        shards,
        mesh=mesh,
        in_specs=(
            P("ctx", "kvh"),
            P(None, "ctx", "kvh"),
            P(None, ("ctx", "kvh"), None),
            P(),
            P(),
            P(None, None, ("ctx", "kvh"), None),
            P(),
            P("kvh", "ctx"),
        ),
        out_specs=(P("ctx", "kvh"), P(None, ("ctx", "kvh"), None), P(None, "ctx")),
        check_vma=False,
    )
```

```python
import jax
import jax.numpy as jnp
from jax import lax
from jax.experimental import pallas as pl
from jax.experimental.pallas import tpu as pltpu
from jax.sharding import PartitionSpec as P

H = 96
KVH = 8
HD = 128
CTX = 32
GROUPS = 4
SAMPLES = 32
PER = H // KVH
PAD = 16
SPAN_ROWS = 128
PRE_ROWS = 64
ROWS = SPAN_ROWS + PRE_ROWS
PREFIX = 2048
LOG2E = 1.4426950408889634
SCALE = HD ** (-0.5) * LOG2E
MASKED = -1e30
LEAST = 2.0**-100
TILE = 512
TILES = 2 * PER * SPAN_ROWS // TILE
CHUNK = 8 * ROWS
HALF = PER * HD
TOTAL = 2 * ROWS + GROUPS * 8 * SAMPLES
PLANE = 8
STACK = 4

MESH = pl.DeviceIdType.MESH
F32 = jnp.float32
BF16 = jnp.bfloat16


def rem(a, n):
    return lax.rem(a, jnp.int32(n))


def dot_t(a, b):
    return lax.dot_general(a, b, (((1,), (1,)), ((), ())), preferred_element_type=F32)


def dot(a, b):
    return jnp.dot(a, b, preferred_element_type=F32)


def remote(src, dst, send, recv, device):
    return pltpu.make_async_remote_copy(
        src_ref=src, dst_ref=dst, send_sem=send, recv_sem=recv, device_id=device, device_id_type=MESH
    )


def kernel(
    limit_ref, suffix_ref, q_ref, span_ref, prefix_ref, private_ref, dq_ref, w_ref,
    out_ref, relaid_out, decode_out,
    kv, kp, vp, dk, dv, acc, top, scores, tops, qs, back, back_in,
    w_buf, dq_buf, qf, priv, suf, bias, msg, inbox, mix_own, mix_all, mix_f, part, parts,
    send, recv, local, kv_send, kv_recv, own_sem, pre_send, pre_recv, pair_send, pair_recv,
    ex_send, ex_recv, part_send, part_recv,
):
    c = lax.axis_index("ctx")
    g = lax.axis_index("kvh")
    limit = limit_ref[0]
    z, x, y = c // 8, rem(c // 2, 4), rem(c, 2)
    mate = c + 1 - 2 * y
    pair = c // 2
    width = 2 * HD

    def lanes(start, size):
        return pl.ds(pl.multiple_of(start, HD), size)

    q_copy = pltpu.make_async_copy(q_ref.at[:, lanes(y * HALF, HALF)], qs.at[1], local.at[2])
    q_copy.start()
    dq_copy = pltpu.make_async_copy(dq_ref.at[:, lanes(g * 2 * HALF, 2 * HALF)], dq_buf, local.at[1])
    dq_copy.start()
    w_copy = pltpu.make_async_copy(w_ref, w_buf, local.at[0])
    w_copy.start()

    barrier = pltpu.get_barrier_semaphore()
    for k in range(1, GROUPS):
        for other in (c, mate):
            pl.semaphore_signal(barrier, inc=1, device_id=(other, rem(g + k, GROUPS)), device_id_type=MESH)

    def greet_ctx(k, carry):
        pl.semaphore_signal(barrier, inc=1, device_id=(rem(c + k, CTX), g), device_id_type=MESH)
        return carry

    lax.fori_loop(1, CTX, greet_ctx, 0)
    mine = jnp.where(y == 0, span_ref[:, :, :HD], span_ref[:, :, HD:])
    kv[y, 0, :, :SPAN_ROWS, :] = mine
    pl.semaphore_wait(barrier, 2 * (GROUPS - 1) + CTX - 1)

    along_y = (mate, g)
    span_copy = remote(
        span_ref.at[:, :, lanes((1 - y) * HD, HD)], kv.at[y, 0, :, :SPAN_ROWS, :],
        pair_send.at[0], pair_recv.at[0], along_y,
    )
    span_copy.start()
    pre_copies = []
    for dy, other_y, other_c in ((1, 1 - y, mate), (0, y, c)):
        for k in range(GROUPS):
            to = rem(g + k, GROUPS)
            src = prefix_ref.at[:, :, lanes((2 * to + other_y) * HD, HD)]
            dst = kv.at[y, 0, :, pl.ds(pl.multiple_of(SPAN_ROWS + g * 16, 16), 16), :]
            if dy == 0 and k == 0:
                copy = pltpu.make_async_copy(src, dst, own_sem.at[0])
            else:
                n = dy * GROUPS + k
                copy = remote(src, dst, pre_send.at[n], pre_recv.at[n], (other_c, to))
                pre_copies.append(copy)
            copy.start()
            if dy == 0 and k == 0:
                pre_own = copy
    query_copy = remote(
        q_ref.at[:, lanes((1 - y) * HALF, HALF)], qs.at[0], pair_send.at[1], pair_recv.at[1], along_y
    )

    def at(z_, x_):
        return z_ * 4 + x_

    def device(p):
        return (2 * p + y, g)

    along_z = (device(at(rem(z + 1, 4), x)), device(at(rem(z + 3, 4), x)))
    along_x = (device(at(z, rem(x + 1, 4))), device(at(z, rem(x + 3, 4))))
    minor = (along_x, along_z)
    major = (along_z, along_x)
    given = {}
    halves = range(2)
    heads = range(2)

    def slot(big, small):
        return big * 4 + small

    def block(e, s, piece):
        return kv.at[e, s] if piece is None else kv.at[e, s, piece : piece + 1]

    def give(e, src, dst, to, piece=None):
        n = len(given)
        given[e, dst, piece] = (n, src)
        remote(block(e, src, piece), block(e, dst, piece), send.at[n], recv.at[n], to).start()

    def take(e, dst, piece=None):
        n, _ = given[e, dst, piece]
        here = block(e, dst, piece)
        remote(here, here, send.at[n], recv.at[n], along_y).wait_recv()

    def both(e, axis, src, dst_next, dst_previous):
        give(e, src, dst_next, axis[e][0])
        give(e, src, dst_previous, axis[e][1])

    def big_step(e, small):
        both(e, major, slot(0, small), slot(3, small), slot(1, small))

    def columns(which):
        return pl.ds(pl.multiple_of(which * width, width), width)

    def rows_of(which, count):
        return pl.ds(pl.multiple_of(which * count, count), count)

    kv_copies = {}

    def exchange(n, pair):
        for k in range(1, GROUPS):
            to = rem(g + k, GROUPS)
            src, dst = pair(to)
            copy = remote(src, dst, kv_send.at[n, k - 1], kv_recv.at[n, k - 1], (c, to))
            copy.start()
            kv_copies[n, k] = copy
        src, dst = pair(g)
        copy = pltpu.make_async_copy(src, dst, own_sem.at[n])
        copy.start()
        kv_copies[n, 0] = copy

    def received(n):
        kv_copies[n, 0].wait()
        for k in range(1, GROUPS):
            kv_copies[n, k].wait_recv()

    exchange(2, lambda to: (private_ref.at[:, :, columns(to)], priv.at[g]))
    query_copy.start()
    exchange(1, lambda to: (span_ref.at[:, rows_of(to, 32), :], relaid_out.at[:, :, columns(g)]))

    span_copy.wait_recv()
    pre_own.wait()
    for copy in pre_copies:
        copy.wait_recv()
    for e in halves:
        both(e, minor, 0, slot(0, 3), slot(0, 1))
    for e in halves:
        big_step(e, 0)

    row = lax.broadcasted_iota(jnp.int32, (SPAN_ROWS, 2 * SPAN_ROWS), 0)
    col = lax.broadcasted_iota(jnp.int32, (SPAN_ROWS, 2 * SPAN_ROWS), 1)
    ones = jnp.ones((SPAN_ROWS, HD), BF16)
    per_tile = TILE // SPAN_ROWS

    def query(t):
        who, first_head = t // (TILES // 2), rem(t, TILES // 2) * per_tile
        return jnp.concatenate(
            [qs[who, :, lanes((first_head + n) * HD, HD)] for n in range(per_tile)], axis=0
        )

    def first(t, carry):
        mine_here = t // (TILES // 2)
        at_y = y * mine_here + (1 - y) * (1 - mine_here)
        allowed = jnp.concatenate([col - SPAN_ROWS * at_y <= row] * per_tile, axis=0)
        keys = jnp.concatenate([kv[0, 0, 0, :SPAN_ROWS, :], kv[1, 0, 0, :SPAN_ROWS, :]], axis=0)
        values = jnp.concatenate(
            [
                jnp.concatenate([kv[0, 0, 1, :SPAN_ROWS, :], ones], axis=1),
                jnp.concatenate([kv[1, 0, 1, :SPAN_ROWS, :], ones], axis=1),
            ],
            axis=0,
        )
        s = jnp.where(allowed, dot_t(query(t), keys) * SCALE, MASKED)
        highest = jnp.broadcast_to(jnp.max(s, axis=1, keepdims=True), (TILE, HD))
        weights = jnp.exp2(s - jnp.concatenate([highest, highest], axis=1)).astype(BF16)
        acc[t] = dot(weights, values)
        top[t] = highest
        return carry

    q_copy.wait()
    lax.fori_loop(TILES // 2, TILES, first, 0)

    for small in (3, 1):
        for e in halves:
            take(e, slot(0, small))
            if small == 3:
                give(e, slot(0, 3), slot(0, 2), minor[e][0], 0)
            else:
                give(e, slot(0, 1), slot(0, 2), minor[e][1], 1)
            big_step(e, small)

    for e in halves:
        take(e, slot(0, 2), 0)
        take(e, slot(0, 2), 1)
        big_step(e, 2)

    qf[...] = jnp.zeros_like(qf)
    dq_copy.wait()
    for j in range(2 * PER):
        start = (j // PER) * SAMPLES * PAD + j % PER
        for level in range(STACK):
            qf[pl.ds(start + level * PAD, PLANE, stride=STACK * PAD), :] = dq_buf[
                level * PLANE : (level + 1) * PLANE, j * HD : (j + 1) * HD
            ].astype(F32)

    def set_suffix(b, carry):
        suf[pl.ds(pl.multiple_of(b * 8, 8), 8), :] = jnp.full((8, HD), suffix_ref[b], jnp.int32)
        return carry

    lax.fori_loop(0, SAMPLES, set_suffix, 0)
    rows = SAMPLES * PAD
    place = lax.broadcasted_iota(jnp.int32, (rows, 2 * HD), 0) >> 4
    key_sample = lax.broadcasted_iota(jnp.int32, (rows, 2 * HD), 1) >> 3
    bias[...] = jnp.where(((place & 3) << 3) + (place >> 2) == key_sample, 0.0, MASKED)

    pre_row = lax.broadcasted_iota(jnp.int32, (PRE_ROWS, HD), 0)

    def put(to_keys, to_values, b, here, ok, key, value, sub):
        count = key.shape[0]
        keep = jnp.where(ok, 1.0, 0.0).astype(BF16)
        drop = jnp.where(ok, 0.0, 1.0).astype(BF16)
        to_keys[b, here : here + count, :] = key * keep + sub * drop
        to_values[b, here : here + count, :HD] = value * keep
        to_values[b, here : here + count, HD:] = keep

    def score(t, b, half):
        q = query(t)
        most = None
        for a in range(0, CHUNK, 2 * HD):
            s = dot_t(q, kp[b, a : a + 2 * HD, :])
            scores[half, :, a : a + 2 * HD] = s
            here = jnp.maximum(s[:, :HD], s[:, HD:])
            most = here if most is None else jnp.maximum(most, here)
        tops[half] = most

    def weigh(t, b, half):
        before = top[t]
        highest = jnp.maximum(
            before, jnp.broadcast_to(jnp.max(tops[half], axis=1, keepdims=True) * SCALE, (TILE, HD))
        )
        rescale = jnp.exp2(before - highest)
        top[t] = highest
        weights = jnp.concatenate(
            [
                jnp.exp2(scores[half, :, a : a + HD] * SCALE - highest).astype(BF16)
                for a in range(0, CHUNK, HD)
            ],
            axis=1,
        )
        acc[t] = acc[t] * jnp.concatenate([rescale, rescale], axis=1) + dot(weights, vp[b, :CHUNK, :])

    def prepare(b, big):
        sub = kv[0, 0, 0, 0:1, :]
        for n in range(4):
            for e in halves:
                dz, dx = (big, n) if e == 0 else (n, big)
                from_pair = at(rem(z + dz, 4), rem(x + dx, 4))
                s = slot(big, n)
                span_ok = jnp.full((SPAN_ROWS, HD), from_pair, jnp.int32) < pair
                pre_ok = (2 * from_pair + e) * PRE_ROWS + pre_row < limit
                here = (2 * n + e) * ROWS
                put(kp, vp, b, here, span_ok, kv[e, s, 0, :SPAN_ROWS, :], kv[e, s, 1, :SPAN_ROWS, :], sub)
                put(kp, vp, b, here + SPAN_ROWS, pre_ok, kv[e, s, 0, SPAN_ROWS:, :], kv[e, s, 1, SPAN_ROWS:, :], sub)

    def run(steps, tile_of, chunk_of):
        def scored(i, half):
            score(tile_of(i), chunk_of(i), half)

        def weighed(i, half):
            weigh(tile_of(i), chunk_of(i), half)

        def two(i, carry):
            scored(2 * i + 1, 1)
            weighed(2 * i, 0)
            scored(2 * i + 2, 0)
            weighed(2 * i + 1, 1)
            return carry

        scored(0, 0)
        lax.fori_loop(0, (steps - 1) // 2, two, 0)
        if steps % 2 == 0:
            scored(steps - 1, 1)
            weighed(steps - 2, 0)
            weighed(steps - 1, 1)
        else:
            weighed(steps - 1, 0)

    def pass_on(*smalls):
        for small in smalls:
            for e in halves:
                if small in (0, 1):
                    take(e, slot(3, small))
                    give(e, slot(3, small), slot(2, small), major[e][0])
                else:
                    take(e, slot(1, small))
                    give(e, slot(1, small), slot(2, small), major[e][1])

    half_tiles = TILES // 2

    def mates(i):
        return rem(i, half_tiles)

    def own(i):
        return half_tiles + rem(i, half_tiles)

    def which(i):
        return i // half_tiles

    prepare(0, 0)
    run(half_tiles, own, lambda i: 0)

    pass_on(0, 3)
    pass_on(1, 2)
    for e in halves:
        take(e, slot(3, 3))
        take(e, slot(3, 2))
    prepare(1, 3)
    run(half_tiles, own, lambda i: 1)

    def message(sums, lse):
        high = [v.astype(BF16).astype(F32) for v in lse]
        middle = [(v - w).astype(BF16).astype(F32) for v, w in zip(lse, high)]
        low = [v - w - u for v, w, u in zip(lse, high, middle)]
        lane = lax.broadcasted_iota(jnp.int32, sums[0].shape, sums[0].ndim - 1)
        stats = jnp.zeros(sums[0].shape, F32)
        for h in heads:
            for n, piece in enumerate((high[h], middle[h], low[h])):
                stats = jnp.where(lane == 3 * h + n, piece, stats)
        return [sums[0].astype(BF16), sums[1].astype(BF16), stats.astype(BF16)]

    def merge(stat, sums, h):
        lse = stat[..., 3 * h : 3 * h + 1] + stat[..., 3 * h + 1 : 3 * h + 2] + stat[..., 3 * h + 2 : 3 * h + 3]
        most = jnp.max(lse, axis=0, keepdims=True)
        weight = jnp.exp2(lse - most)
        total = jnp.sum(weight, axis=0)
        return jnp.sum(weight * sums.astype(F32), axis=0) / total

    received(2)
    row_in = lax.broadcasted_iota(jnp.int32, (8 * SAMPLES, HD), 0) & 7
    partial, partial_lse = [], []
    for h in heads:
        cols = slice(h * HD, (h + 1) * HD)
        sub = span_ref[0, 0:1, cols]
        held = jnp.full((SPAN_ROWS, HD), y, jnp.int32) == h
        for e in halves:
            pre_ok = (2 * pair + e) * PRE_ROWS + pre_row < jnp.where(y == h, limit, 0)
            put(dk, dv, h, e * ROWS, held, kv[e, 0, 0, :SPAN_ROWS, :], kv[e, 0, 1, :SPAN_ROWS, :], sub)
            put(dk, dv, h, e * ROWS + SPAN_ROWS, pre_ok, kv[e, 0, 0, SPAN_ROWS:, :], kv[e, 0, 1, SPAN_ROWS:, :], sub)
        for s in range(GROUPS):
            ok = (c * GROUPS + s) * 8 + row_in < suf[...]
            put(dk, dv, h, 2 * ROWS + s * 8 * SAMPLES, ok, priv[s, 0, :, cols], priv[s, 1, :, cols], sub)
        q = qf[h * rows : (h + 1) * rows, :].astype(BF16)
        most = None
        for start, count in [(a, HD) for a in range(0, 2 * ROWS, HD)] + [(2 * ROWS + s * 256, 256) for s in range(GROUPS)]:
            s = dot_t(q, dk[h, start : start + count, :]) * SCALE
            if count == 256:
                s = s + bias[...]
            scores[h, :, start : start + count] = s
            here = jnp.maximum(s[:, :HD], s[:, HD:]) if count == 256 else s
            most = here if most is None else jnp.maximum(most, here)
        most = jnp.broadcast_to(jnp.max(most, axis=1, keepdims=True), (rows, HD))
        weights = jnp.concatenate(
            [jnp.exp2(scores[h, :, a : a + HD] - most).astype(BF16) for a in range(0, TOTAL, HD)], axis=1
        )
        both_sums = dot(weights, dv[h, :TOTAL, :])
        sum_here = jnp.maximum(both_sums[:, HD:], LEAST)
        partial.append(both_sums[:, :HD] / sum_here)
        partial_lse.append(most + jnp.log2(sum_here))
    for n, piece in enumerate(message(partial, partial_lse)):
        msg[:, n, :, :] = piece.reshape(SAMPLES, PAD, HD)

    def place_of(ctx):
        return rem(ctx, PLANE) * STACK + ctx // PLANE

    def in_copy(k):
        to = rem(c + k, CTX)
        return remote(msg.at[place_of(to)], inbox.at[k], ex_send.at[0], ex_recv.at[0], (to, g))

    def mix_copy(k):
        to = rem(c + k, CTX)
        return remote(mix_own, mix_all.at[place_of(c)], ex_send.at[1], ex_recv.at[1], (to, g))

    def every(act):
        def one(k, carry):
            act(k)
            return carry

        lax.fori_loop(1, CTX, one, 0)

    every(lambda k: in_copy(k).start())
    inbox[0] = msg[place_of(c)]

    query_copy.wait_recv()
    lax.fori_loop(0, half_tiles, first, 0)
    run(TILES, mates, which)

    others = inbox.at[1:]
    remote(others, others, ex_send.at[0], ex_recv.at[0], along_y).wait()
    stat = inbox[:, 2, :, :].astype(F32)
    for h in heads:
        mix_own[h] = merge(stat, inbox[:, h, :, :], h).astype(BF16)
    every(lambda k: mix_copy(k).start())
    mix_all[place_of(c)] = mix_own[...]

    for e in halves:
        for small in range(4):
            if small < 2:
                take(e, slot(1, small))
            take(e, slot(2, small))
    prepare(0, 1)
    prepare(1, 2)
    run(TILES, mates, which)

    for j in range(PER):
        t, r = j * SPAN_ROWS // TILE, j * SPAN_ROWS % TILE
        here = slice(r, r + SPAN_ROWS)
        back[:, j * HD : (j + 1) * HD] = (acc[t, here, :HD] / acc[t, here, HD:]).astype(BF16)
    back_copy = remote(back, back_in, pair_send.at[2], pair_recv.at[2], along_y)
    back_copy.start()

    others = mix_all.at[1:]
    remote(others, others, ex_send.at[1], ex_recv.at[1], along_y).wait()
    mix_f[...] = mix_all[...].astype(F32).reshape(SAMPLES * 2 * PAD, HD)
    w_copy.wait()
    product = jnp.zeros((SAMPLES, w_buf.shape[1]), F32)
    for j in range(2 * PER):
        start = (j // PER) * PAD + j % PER
        a = jnp.concatenate(
            [
                mix_f[pl.ds(start + n * 2 * PAD, PLANE, stride=STACK * 2 * PAD), :]
                for n in range(STACK)
            ],
            axis=0,
        ).astype(BF16)
        product = product + dot(a, w_buf[j * HD : (j + 1) * HD, :])
    part[...] = product
    part_copies = []
    for k in range(1, GROUPS):
        to = rem(g + k, GROUPS)
        copy = remote(part, parts.at[g], part_send.at[k - 1], part_recv.at[k - 1], (c, to))
        copy.start()
        part_copies.append(copy)
    parts[g] = product

    run(TILES, own, which)

    for j in range(PER):
        t, r = half_tiles + j * SPAN_ROWS // TILE, j * SPAN_ROWS % TILE
        here = slice(r, r + SPAN_ROWS)
        out_ref[:, lanes(y * HALF + j * HD, HD)] = acc[t, here, :HD] / acc[t, here, HD:]
    back_copy.wait()
    out_ref[:, lanes((1 - y) * HALF, HALF)] = back_in[...].astype(F32)

    for copy in part_copies:
        copy.wait()
    decode_out[...] = (parts[0] + parts[1]) + (parts[2] + parts[3])
    received(1)
    for (n, k), copy in kv_copies.items():
        if k:
            copy.wait_send()
    span_copy.wait_send()
    query_copy.wait_send()
    for copy in pre_copies:
        copy.wait_send()
    for (e, _, piece), (n, src) in given.items():
        there = block(e, src, piece)
        remote(there, there, send.at[n], recv.at[n], along_y).wait_send()


def shards(
    span_queries,
    span_keyvals,
    prefix_keyvals,
    offset,
    decode_queries,
    private_keyvals,
    suffix_lengths,
    out_weight,
):
    vmem = pl.BlockSpec(memory_space=pltpu.VMEM)
    smem = pl.BlockSpec(memory_space=pltpu.SMEM)
    hbm = pl.BlockSpec(memory_space=pl.ANY)
    dma = pltpu.SemaphoreType.DMA
    group = 2 * PER * HD
    wide = out_weight.shape[1]
    private = private_keyvals.reshape(2, SAMPLES * 8, KVH * HD)
    return pl.pallas_call(
        kernel,
        out_shape=(
            jax.ShapeDtypeStruct((SPAN_ROWS, group), F32),
            jax.ShapeDtypeStruct((2, SPAN_ROWS // GROUPS, KVH * HD), BF16),
            jax.ShapeDtypeStruct((SAMPLES, wide), F32),
        ),
        in_specs=[smem, smem, hbm, vmem, vmem, hbm, hbm, hbm],
        out_specs=(vmem, vmem, vmem),
        scratch_shapes=[
            pltpu.VMEM((2, CTX // 2, 2, ROWS, HD), BF16),
            pltpu.VMEM((2, CHUNK, HD), BF16),
            pltpu.VMEM((2, CHUNK, 2 * HD), BF16),
            pltpu.VMEM((2, TOTAL, HD), BF16),
            pltpu.VMEM((2, TOTAL, 2 * HD), BF16),
            pltpu.VMEM((TILES, TILE, 2 * HD), F32),
            pltpu.VMEM((TILES, TILE, HD), F32),
            pltpu.VMEM((2, TILE, CHUNK), F32),
            pltpu.VMEM((2, TILE, HD), F32),
            pltpu.VMEM((2, SPAN_ROWS, group // 2), BF16),
            pltpu.VMEM((SPAN_ROWS, group // 2), BF16),
            pltpu.VMEM((SPAN_ROWS, group // 2), BF16),
            pltpu.VMEM((group, wide), BF16),
            pltpu.VMEM((SAMPLES, group), BF16),
            pltpu.VMEM((2 * SAMPLES * PAD, HD), F32),
            pltpu.VMEM((GROUPS, 2, SAMPLES * 8, 2 * HD), BF16),
            pltpu.VMEM((SAMPLES * 8, HD), jnp.int32),
            pltpu.VMEM((SAMPLES * PAD, 2 * HD), F32),
            pltpu.VMEM((SAMPLES, 3, PAD, HD), BF16),
            pltpu.VMEM((CTX, 3, PAD, HD), BF16),
            pltpu.VMEM((2, PAD, HD), BF16),
            pltpu.VMEM((SAMPLES, 2, PAD, HD), BF16),
            pltpu.VMEM((SAMPLES * 2 * PAD, HD), F32),
            pltpu.VMEM((SAMPLES, wide), F32),
            pltpu.VMEM((GROUPS, SAMPLES, wide), F32),
            dma((40,)), dma((40,)), dma((3,)),
            dma((3, GROUPS - 1)), dma((3, GROUPS - 1)), dma((3,)),
            dma((2 * GROUPS,)), dma((2 * GROUPS,)), dma((3,)), dma((3,)),
            dma((2,)), dma((2,)), dma((GROUPS - 1,)), dma((GROUPS - 1,)),
        ],
        compiler_params=pltpu.CompilerParams(
            collective_id=0, has_side_effects=True, vmem_limit_bytes=60 * 1024 * 1024
        ),
        name="attention",
    )(offset, suffix_lengths, span_queries, span_keyvals, prefix_keyvals, private, decode_queries, out_weight)


def solution(mesh):
    return jax.shard_map(
        shards,
        mesh=mesh,
        in_specs=(
            P("ctx", "kvh"),
            P(None, "ctx", "kvh"),
            P(None, ("ctx", "kvh"), None),
            P(),
            P(),
            P(None, None, ("ctx", "kvh"), None),
            P(),
            P("kvh", "ctx"),
        ),
        out_specs=(P("ctx", "kvh"), P(None, ("ctx", "kvh"), None), P(None, "ctx")),
        check_vma=False,
    )
```

```python
import jax
import jax.numpy as jnp
from jax import lax
from jax.experimental import pallas as pl
from jax.experimental.pallas import tpu as pltpu
from jax.sharding import PartitionSpec as P

H = 96
KVH = 8
HD = 128
CTX = 32
GROUPS = 4
SAMPLES = 32
PER = H // KVH
PAD = 16
SPAN_ROWS = 128
PRE_ROWS = 64
ROWS = SPAN_ROWS + PRE_ROWS
PREFIX = 2048
LOG2E = 1.4426950408889634
SCALE = HD ** (-0.5) * LOG2E
MASKED = -1e30
LEAST = 2.0**-100
TILE = 768
TILES = 2 * PER * SPAN_ROWS // TILE
CHUNK = 8 * ROWS
HALF = PER * HD
TOTAL = 2 * ROWS + GROUPS * 8 * SAMPLES
PLANE = 8
STACK = 4

MESH = pl.DeviceIdType.MESH
F32 = jnp.float32
BF16 = jnp.bfloat16


def rem(a, n):
    return lax.rem(a, jnp.int32(n))


def dot_t(a, b):
    return lax.dot_general(a, b, (((1,), (1,)), ((), ())), preferred_element_type=F32)


def dot(a, b):
    return jnp.dot(a, b, preferred_element_type=F32)


def remote(src, dst, send, recv, device):
    return pltpu.make_async_remote_copy(
        src_ref=src, dst_ref=dst, send_sem=send, recv_sem=recv, device_id=device, device_id_type=MESH
    )


def kernel(
    limit_ref, suffix_ref, q_ref, span_ref, prefix_ref, private_ref, dq_ref, w_ref,
    out_ref, relaid_out, decode_out,
    kv, kp, vp, dk, dv, acc, top, scores, tops, qs, back,
    w_buf, dq_buf, qf, priv, suf, bias, msg, inbox, mix_own, mix_all, mix_f, part, parts,
    send, recv, local, kv_send, kv_recv, own_sem, pre_send, pre_recv, pair_send, pair_recv,
    ex_send, ex_recv, part_send, part_recv,
):
    c = lax.axis_index("ctx")
    g = lax.axis_index("kvh")
    limit = limit_ref[0]
    z, x, y = c // 8, rem(c // 2, 4), rem(c, 2)
    mate = c + 1 - 2 * y
    pair = c // 2
    width = 2 * HD

    def lanes(start, size):
        return pl.ds(pl.multiple_of(start, HD), size)

    q_copy = pltpu.make_async_copy(q_ref.at[:, lanes(y * HALF, HALF)], qs.at[1], local.at[2])
    q_copy.start()
    dq_copy = pltpu.make_async_copy(dq_ref.at[:, lanes(g * 2 * HALF, 2 * HALF)], dq_buf, local.at[1])
    dq_copy.start()
    w_copy = pltpu.make_async_copy(w_ref, w_buf, local.at[0])
    w_copy.start()

    barrier = pltpu.get_barrier_semaphore()
    for k in range(1, GROUPS):
        for other in (c, mate):
            pl.semaphore_signal(barrier, inc=1, device_id=(other, rem(g + k, GROUPS)), device_id_type=MESH)

    def greet_ctx(k, carry):
        pl.semaphore_signal(barrier, inc=1, device_id=(rem(c + k, CTX), g), device_id_type=MESH)
        return carry

    lax.fori_loop(1, CTX, greet_ctx, 0)
    mine = jnp.where(y == 0, span_ref[:, :, :HD], span_ref[:, :, HD:])
    kv[y, 0, :, :SPAN_ROWS, :] = mine
    pl.semaphore_wait(barrier, 2 * (GROUPS - 1) + CTX - 1)

    along_y = (mate, g)
    pre_copies = []
    for dy, other_y, other_c in ((1, 1 - y, mate), (0, y, c)):
        for k in range(GROUPS):
            to = rem(g + k, GROUPS)
            src = prefix_ref.at[:, :, lanes((2 * to + other_y) * HD, HD)]
            dst = kv.at[y, 0, :, pl.ds(pl.multiple_of(SPAN_ROWS + g * 16, 16), 16), :]
            if dy == 0 and k == 0:
                copy = pltpu.make_async_copy(src, dst, own_sem.at[0])
            else:
                n = dy * GROUPS + k
                copy = remote(src, dst, pre_send.at[n], pre_recv.at[n], (other_c, to))
                pre_copies.append(copy)
            copy.start()
            if dy == 0 and k == 0:
                pre_own = copy
    span_copy = remote(
        span_ref.at[:, :, lanes((1 - y) * HD, HD)], kv.at[y, 0, :, :SPAN_ROWS, :],
        pair_send.at[0], pair_recv.at[0], along_y,
    )
    span_copy.start()
    query_copy = remote(
        q_ref.at[:, lanes((1 - y) * HALF, HALF)], qs.at[0], pair_send.at[1], pair_recv.at[1], along_y
    )

    def at(z_, x_):
        return z_ * 4 + x_

    def device(p):
        return (2 * p + y, g)

    along_z = (device(at(rem(z + 1, 4), x)), device(at(rem(z + 3, 4), x)))
    along_x = (device(at(z, rem(x + 1, 4))), device(at(z, rem(x + 3, 4))))
    minor = (along_x, along_z)
    major = (along_z, along_x)
    given = {}
    halves = range(2)
    heads = range(2)

    def slot(big, small):
        return big * 4 + small

    def block(e, s, piece):
        return kv.at[e, s] if piece is None else kv.at[e, s, piece : piece + 1]

    def give(e, src, dst, to, piece=None):
        n = len(given)
        given[e, dst, piece] = (n, src)
        remote(block(e, src, piece), block(e, dst, piece), send.at[n], recv.at[n], to).start()

    def take(e, dst, piece=None):
        n, _ = given[e, dst, piece]
        here = block(e, dst, piece)
        remote(here, here, send.at[n], recv.at[n], along_y).wait_recv()

    def both(e, axis, src, dst_next, dst_previous):
        give(e, src, dst_next, axis[e][0])
        give(e, src, dst_previous, axis[e][1])

    def big_step(e, small):
        both(e, major, slot(0, small), slot(3, small), slot(1, small))

    def columns(which):
        return pl.ds(pl.multiple_of(which * width, width), width)

    def rows_of(which, count):
        return pl.ds(pl.multiple_of(which * count, count), count)

    kv_copies = {}

    def exchange(n, pair):
        for k in range(1, GROUPS):
            to = rem(g + k, GROUPS)
            src, dst = pair(to)
            copy = remote(src, dst, kv_send.at[n, k - 1], kv_recv.at[n, k - 1], (c, to))
            copy.start()
            kv_copies[n, k] = copy
        src, dst = pair(g)
        copy = pltpu.make_async_copy(src, dst, own_sem.at[n])
        copy.start()
        kv_copies[n, 0] = copy

    def received(n):
        kv_copies[n, 0].wait()
        for k in range(1, GROUPS):
            kv_copies[n, k].wait_recv()

    exchange(2, lambda to: (private_ref.at[:, :, columns(to)], priv.at[g]))
    query_copy.start()
    exchange(1, lambda to: (span_ref.at[:, rows_of(to, 32), :], relaid_out.at[:, :, columns(g)]))

    span_copy.wait_recv()
    pre_own.wait()
    for copy in pre_copies:
        copy.wait_recv()
    for e in halves:
        both(e, minor, 0, slot(0, 3), slot(0, 1))
    for e in halves:
        big_step(e, 0)

    row = lax.broadcasted_iota(jnp.int32, (SPAN_ROWS, 2 * SPAN_ROWS), 0)
    col = lax.broadcasted_iota(jnp.int32, (SPAN_ROWS, 2 * SPAN_ROWS), 1)
    ones = jnp.ones((SPAN_ROWS, HD), BF16)
    per_tile = TILE // SPAN_ROWS

    def query(t):
        who, first_head = t // (TILES // 2), rem(t, TILES // 2) * per_tile
        return jnp.concatenate(
            [qs[who, :, lanes((first_head + n) * HD, HD)] for n in range(per_tile)], axis=0
        )

    def first(t, carry):
        mine_here = t // (TILES // 2)
        at_y = y * mine_here + (1 - y) * (1 - mine_here)
        allowed = jnp.concatenate([col - SPAN_ROWS * at_y <= row] * per_tile, axis=0)
        keys = jnp.concatenate([kv[0, 0, 0, :SPAN_ROWS, :], kv[1, 0, 0, :SPAN_ROWS, :]], axis=0)
        values = jnp.concatenate(
            [
                jnp.concatenate([kv[0, 0, 1, :SPAN_ROWS, :], ones], axis=1),
                jnp.concatenate([kv[1, 0, 1, :SPAN_ROWS, :], ones], axis=1),
            ],
            axis=0,
        )
        s = jnp.where(allowed, dot_t(query(t), keys) * SCALE, MASKED)
        highest = jnp.broadcast_to(jnp.max(s, axis=1, keepdims=True), (TILE, HD))
        weights = jnp.exp2(s - jnp.concatenate([highest, highest], axis=1)).astype(BF16)
        acc[t] = dot(weights, values)
        top[t] = highest
        return carry

    q_copy.wait()
    lax.fori_loop(TILES // 2, TILES, first, 0)

    for small in (3, 1):
        for e in halves:
            take(e, slot(0, small))
            if small == 3:
                give(e, slot(0, 3), slot(0, 2), minor[e][0], 0)
            else:
                give(e, slot(0, 1), slot(0, 2), minor[e][1], 1)
            big_step(e, small)

    for e in halves:
        take(e, slot(0, 2), 0)
        take(e, slot(0, 2), 1)
        big_step(e, 2)

    pre_row = lax.broadcasted_iota(jnp.int32, (PRE_ROWS, HD), 0)

    def put(to_keys, to_values, b, here, ok, key, value, sub):
        count = key.shape[0]
        keep = jnp.where(ok, 1.0, 0.0).astype(BF16)
        drop = jnp.where(ok, 0.0, 1.0).astype(BF16)
        to_keys[b, here : here + count, :] = key * keep + sub * drop
        to_values[b, here : here + count, :HD] = value * keep
        to_values[b, here : here + count, HD:] = keep

    def score(t, b, half):
        q = query(t)
        most = None
        for a in range(0, CHUNK, 2 * HD):
            s = dot_t(q, kp[b, a : a + 2 * HD, :])
            scores[half, :, a : a + 2 * HD] = s
            here = jnp.maximum(s[:, :HD], s[:, HD:])
            most = here if most is None else jnp.maximum(most, here)
        tops[half] = most

    def weigh(t, b, half):
        before = top[t]
        highest = jnp.maximum(
            before, jnp.broadcast_to(jnp.max(tops[half], axis=1, keepdims=True) * SCALE, (TILE, HD))
        )
        rescale = jnp.exp2(before - highest)
        top[t] = highest
        weights = jnp.concatenate(
            [
                jnp.exp2(scores[half, :, a : a + HD] * SCALE - highest).astype(BF16)
                for a in range(0, CHUNK, HD)
            ],
            axis=1,
        )
        acc[t] = acc[t] * jnp.concatenate([rescale, rescale], axis=1) + dot(weights, vp[b, :CHUNK, :])

    def prepare(b, big):
        sub = kv[0, 0, 0, 0:1, :]
        for n in range(4):
            for e in halves:
                dz, dx = (big, n) if e == 0 else (n, big)
                from_pair = at(rem(z + dz, 4), rem(x + dx, 4))
                s = slot(big, n)
                span_ok = jnp.full((SPAN_ROWS, HD), from_pair, jnp.int32) < pair
                pre_ok = (2 * from_pair + e) * PRE_ROWS + pre_row < limit
                here = (2 * n + e) * ROWS
                put(kp, vp, b, here, span_ok, kv[e, s, 0, :SPAN_ROWS, :], kv[e, s, 1, :SPAN_ROWS, :], sub)
                put(kp, vp, b, here + SPAN_ROWS, pre_ok, kv[e, s, 0, SPAN_ROWS:, :], kv[e, s, 1, SPAN_ROWS:, :], sub)

    def run(steps, tile_of, chunk_of):
        def scored(i, half):
            score(tile_of(i), chunk_of(i), half)

        def weighed(i, half):
            weigh(tile_of(i), chunk_of(i), half)

        def two(i, carry):
            scored(2 * i + 1, 1)
            weighed(2 * i, 0)
            scored(2 * i + 2, 0)
            weighed(2 * i + 1, 1)
            return carry

        scored(0, 0)
        lax.fori_loop(0, (steps - 1) // 2, two, 0)
        if steps % 2 == 0:
            scored(steps - 1, 1)
            weighed(steps - 2, 0)
            weighed(steps - 1, 1)
        else:
            weighed(steps - 1, 0)

    def pass_on(*smalls):
        for small in smalls:
            for e in halves:
                if small in (0, 1):
                    take(e, slot(3, small))
                    give(e, slot(3, small), slot(2, small), major[e][0])
                else:
                    take(e, slot(1, small))
                    give(e, slot(1, small), slot(2, small), major[e][1])

    half_tiles = TILES // 2

    def mates(i):
        return rem(i, half_tiles)

    def own(i):
        return half_tiles + rem(i, half_tiles)

    def which(i):
        return i // half_tiles

    prepare(0, 0)
    run(half_tiles, own, lambda i: 0)

    pass_on(0, 3)

    qf[...] = jnp.zeros_like(qf)
    dq_copy.wait()
    for j in range(2 * PER):
        start = (j // PER) * SAMPLES * PAD + j % PER
        for level in range(STACK):
            qf[pl.ds(start + level * PAD, PLANE, stride=STACK * PAD), :] = dq_buf[
                level * PLANE : (level + 1) * PLANE, j * HD : (j + 1) * HD
            ].astype(F32)

    def set_suffix(b, carry):
        suf[pl.ds(pl.multiple_of(b * 8, 8), 8), :] = jnp.full((8, HD), suffix_ref[b], jnp.int32)
        return carry

    lax.fori_loop(0, SAMPLES, set_suffix, 0)
    rows = SAMPLES * PAD
    place = lax.broadcasted_iota(jnp.int32, (rows, 2 * HD), 0) >> 4
    key_sample = lax.broadcasted_iota(jnp.int32, (rows, 2 * HD), 1) >> 3
    bias[...] = jnp.where(((place & 3) << 3) + (place >> 2) == key_sample, 0.0, MASKED)

    pass_on(1, 2)
    for e in halves:
        take(e, slot(3, 3))
        take(e, slot(3, 2))
    prepare(1, 3)
    run(half_tiles, own, lambda i: 1)

    def message(sums, lse):
        high = [v.astype(BF16).astype(F32) for v in lse]
        middle = [(v - w).astype(BF16).astype(F32) for v, w in zip(lse, high)]
        low = [v - w - u for v, w, u in zip(lse, high, middle)]
        lane = lax.broadcasted_iota(jnp.int32, sums[0].shape, sums[0].ndim - 1)
        stats = jnp.zeros(sums[0].shape, F32)
        for h in heads:
            for n, piece in enumerate((high[h], middle[h], low[h])):
                stats = jnp.where(lane == 3 * h + n, piece, stats)
        return [sums[0].astype(BF16), sums[1].astype(BF16), stats.astype(BF16)]

    def merge(stat, sums, h):
        lse = stat[..., 3 * h : 3 * h + 1] + stat[..., 3 * h + 1 : 3 * h + 2] + stat[..., 3 * h + 2 : 3 * h + 3]
        most = jnp.max(lse, axis=0, keepdims=True)
        weight = jnp.exp2(lse - most)
        total = jnp.sum(weight, axis=0)
        return jnp.sum(weight * sums.astype(F32), axis=0) / total

    received(2)
    row_in = lax.broadcasted_iota(jnp.int32, (8 * SAMPLES, HD), 0) & 7
    partial, partial_lse = [], []
    for h in heads:
        cols = slice(h * HD, (h + 1) * HD)
        sub = span_ref[0, 0:1, cols]
        held = jnp.full((SPAN_ROWS, HD), y, jnp.int32) == h
        for e in halves:
            pre_ok = (2 * pair + e) * PRE_ROWS + pre_row < jnp.where(y == h, limit, 0)
            put(dk, dv, h, e * ROWS, held, kv[e, 0, 0, :SPAN_ROWS, :], kv[e, 0, 1, :SPAN_ROWS, :], sub)
            put(dk, dv, h, e * ROWS + SPAN_ROWS, pre_ok, kv[e, 0, 0, SPAN_ROWS:, :], kv[e, 0, 1, SPAN_ROWS:, :], sub)
        for s in range(GROUPS):
            ok = (c * GROUPS + s) * 8 + row_in < suf[...]
            put(dk, dv, h, 2 * ROWS + s * 8 * SAMPLES, ok, priv[s, 0, :, cols], priv[s, 1, :, cols], sub)
        q = qf[h * rows : (h + 1) * rows, :].astype(BF16)
        most = None
        for start, count in [(a, HD) for a in range(0, 2 * ROWS, HD)] + [(2 * ROWS + s * 256, 256) for s in range(GROUPS)]:
            s = dot_t(q, dk[h, start : start + count, :]) * SCALE
            if count == 256:
                s = s + bias[...]
            scores[h, :rows, start : start + count] = s
            here = jnp.maximum(s[:, :HD], s[:, HD:]) if count == 256 else s
            most = here if most is None else jnp.maximum(most, here)
        most = jnp.broadcast_to(jnp.max(most, axis=1, keepdims=True), (rows, HD))
        weights = jnp.concatenate(
            [jnp.exp2(scores[h, :rows, a : a + HD] - most).astype(BF16) for a in range(0, TOTAL, HD)], axis=1
        )
        both_sums = dot(weights, dv[h, :TOTAL, :])
        sum_here = jnp.maximum(both_sums[:, HD:], LEAST)
        partial.append(both_sums[:, :HD] / sum_here)
        partial_lse.append(most + jnp.log2(sum_here))
    for n, piece in enumerate(message(partial, partial_lse)):
        msg[:, n, :, :] = piece.reshape(SAMPLES, PAD, HD)

    def place_of(ctx):
        return rem(ctx, PLANE) * STACK + ctx // PLANE

    def in_copy(k):
        to = rem(c + k, CTX)
        return remote(msg.at[place_of(to)], inbox.at[k], ex_send.at[0], ex_recv.at[0], (to, g))

    def mix_copy(k):
        to = rem(c + k, CTX)
        return remote(mix_own, mix_all.at[place_of(c)], ex_send.at[1], ex_recv.at[1], (to, g))

    def every(act):
        def one(k, carry):
            act(k)
            return carry

        lax.fori_loop(1, CTX, one, 0)

    every(lambda k: in_copy(k).start())
    inbox[0] = msg[place_of(c)]

    query_copy.wait_recv()
    lax.fori_loop(0, half_tiles, first, 0)
    run(TILES, mates, which)

    others = inbox.at[1:]
    remote(others, others, ex_send.at[0], ex_recv.at[0], along_y).wait()
    stat = inbox[:, 2, :, :].astype(F32)
    for h in heads:
        mix_own[h] = merge(stat, inbox[:, h, :, :], h).astype(BF16)
    every(lambda k: mix_copy(k).start())
    mix_all[place_of(c)] = mix_own[...]

    for e in halves:
        for small in range(4):
            if small < 2:
                take(e, slot(1, small))
            take(e, slot(2, small))
    prepare(0, 1)
    prepare(1, 2)
    run(TILES, mates, which)

    for j in range(PER):
        t, r = j * SPAN_ROWS // TILE, j * SPAN_ROWS % TILE
        here = slice(r, r + SPAN_ROWS)
        back[:, j * HD : (j + 1) * HD] = (acc[t, here, :HD] / acc[t, here, HD:]).astype(BF16)
    back_copy = remote(back, out_ref.at[:, lanes(y * HALF, HALF)], pair_send.at[2], pair_recv.at[2], along_y)
    back_copy.start()

    others = mix_all.at[1:]
    remote(others, others, ex_send.at[1], ex_recv.at[1], along_y).wait()
    mix_f[...] = mix_all[...].astype(F32).reshape(SAMPLES * 2 * PAD, HD)
    w_copy.wait()
    product = jnp.zeros((SAMPLES, w_buf.shape[1]), F32)
    for j in range(2 * PER):
        start = (j // PER) * PAD + j % PER
        a = jnp.concatenate(
            [
                mix_f[pl.ds(start + n * 2 * PAD, PLANE, stride=STACK * 2 * PAD), :]
                for n in range(STACK)
            ],
            axis=0,
        ).astype(BF16)
        product = product + dot(a, w_buf[j * HD : (j + 1) * HD, :])
    part[...] = product
    part_copies = []
    for k in range(1, GROUPS):
        to = rem(g + k, GROUPS)
        copy = remote(part, parts.at[g], part_send.at[k - 1], part_recv.at[k - 1], (c, to))
        copy.start()
        part_copies.append(copy)
    parts[g] = product

    run(TILES, own, which)

    for j in range(PER):
        t, r = half_tiles + j * SPAN_ROWS // TILE, j * SPAN_ROWS % TILE
        here = slice(r, r + SPAN_ROWS)
        out_ref[:, lanes(y * HALF + j * HD, HD)] = (acc[t, here, :HD] / acc[t, here, HD:]).astype(BF16)
    back_copy.wait()

    for copy in part_copies:
        copy.wait()
    decode_out[...] = (parts[0] + parts[1]) + (parts[2] + parts[3])
    received(1)
    for (n, k), copy in kv_copies.items():
        if k:
            copy.wait_send()
    span_copy.wait_send()
    query_copy.wait_send()
    for copy in pre_copies:
        copy.wait_send()
    for (e, _, piece), (n, src) in given.items():
        there = block(e, src, piece)
        remote(there, there, send.at[n], recv.at[n], along_y).wait_send()


def shards(
    span_queries,
    span_keyvals,
    prefix_keyvals,
    offset,
    decode_queries,
    private_keyvals,
    suffix_lengths,
    out_weight,
):
    vmem = pl.BlockSpec(memory_space=pltpu.VMEM)
    smem = pl.BlockSpec(memory_space=pltpu.SMEM)
    hbm = pl.BlockSpec(memory_space=pl.ANY)
    dma = pltpu.SemaphoreType.DMA
    group = 2 * PER * HD
    wide = out_weight.shape[1]
    private = private_keyvals.reshape(2, SAMPLES * 8, KVH * HD)
    span_attention, relaid_span, decode_output = pl.pallas_call(
        kernel,
        out_shape=(
            jax.ShapeDtypeStruct((SPAN_ROWS, group), BF16),
            jax.ShapeDtypeStruct((2, SPAN_ROWS // GROUPS, KVH * HD), BF16),
            jax.ShapeDtypeStruct((SAMPLES, wide), F32),
        ),
        in_specs=[smem, smem, hbm, vmem, vmem, hbm, hbm, hbm],
        out_specs=(vmem, vmem, vmem),
        scratch_shapes=[
            pltpu.VMEM((2, CTX // 2, 2, ROWS, HD), BF16),
            pltpu.VMEM((2, CHUNK, HD), BF16),
            pltpu.VMEM((2, CHUNK, 2 * HD), BF16),
            pltpu.VMEM((2, TOTAL, HD), BF16),
            pltpu.VMEM((2, TOTAL, 2 * HD), BF16),
            pltpu.VMEM((TILES, TILE, 2 * HD), F32),
            pltpu.VMEM((TILES, TILE, HD), F32),
            pltpu.VMEM((2, TILE, CHUNK), F32),
            pltpu.VMEM((2, TILE, HD), F32),
            pltpu.VMEM((2, SPAN_ROWS, group // 2), BF16),
            pltpu.VMEM((SPAN_ROWS, group // 2), BF16),
            pltpu.VMEM((group, wide), BF16),
            pltpu.VMEM((SAMPLES, group), BF16),
            pltpu.VMEM((2 * SAMPLES * PAD, HD), F32),
            pltpu.VMEM((GROUPS, 2, SAMPLES * 8, 2 * HD), BF16),
            pltpu.VMEM((SAMPLES * 8, HD), jnp.int32),
            pltpu.VMEM((SAMPLES * PAD, 2 * HD), F32),
            pltpu.VMEM((SAMPLES, 3, PAD, HD), BF16),
            pltpu.VMEM((CTX, 3, PAD, HD), BF16),
            pltpu.VMEM((2, PAD, HD), BF16),
            pltpu.VMEM((SAMPLES, 2, PAD, HD), BF16),
            pltpu.VMEM((SAMPLES * 2 * PAD, HD), F32),
            pltpu.VMEM((SAMPLES, wide), F32),
            pltpu.VMEM((GROUPS, SAMPLES, wide), F32),
            dma((40,)), dma((40,)), dma((3,)),
            dma((3, GROUPS - 1)), dma((3, GROUPS - 1)), dma((3,)),
            dma((2 * GROUPS,)), dma((2 * GROUPS,)), dma((3,)), dma((3,)),
            dma((2,)), dma((2,)), dma((GROUPS - 1,)), dma((GROUPS - 1,)),
        ],
        compiler_params=pltpu.CompilerParams(
            collective_id=0, has_side_effects=True, vmem_limit_bytes=60 * 1024 * 1024
        ),
        name="attention",
    )(offset, suffix_lengths, span_queries, span_keyvals, prefix_keyvals, private, decode_queries, out_weight)
    return (span_attention.astype(F32), relaid_span, decode_output)


def solution(mesh):
    return jax.shard_map(
        shards,
        mesh=mesh,
        in_specs=(
            P("ctx", "kvh"),
            P(None, "ctx", "kvh"),
            P(None, ("ctx", "kvh"), None),
            P(),
            P(),
            P(None, None, ("ctx", "kvh"), None),
            P(),
            P("kvh", "ctx"),
        ),
        out_specs=(P("ctx", "kvh"), P(None, ("ctx", "kvh"), None), P(None, "ctx")),
        check_vma=False,
    )
```
